128 devices in a mesh: rep: 2 (over z_hi), zero: 8 (over y, z_lo), ctx: 8 (over x, core).
Axes of the slice: x: 4, y: 4, z: 4 (z_hi: 2, z_lo: 2; z = z_hi * 2 + z_lo), core: 2. Of those that a mesh axis runs over, the one named last changes fastest.
Arguments:
- tokens: bfloat16 [32768, 1024], P(('rep', 'zero', 'ctx')), may hold values from -6 to 6
- cotangent: bfloat16 [32768, 1024], P(('rep', 'zero', 'ctx')), may hold values from -6 to 6
- seq_lengths: int32 [16, 2], P(('rep', 'zero')), may hold values from 1 to 1920, as said below
- master_qkv: float32 [1024, 3072], P('zero'), may hold values from -0.1875 to 0.1875
- master_dense: float32 [1024, 1024], P('zero'), may hold values from -1.5 to 1.5
- master_in: float32 [1024, 4096], P('zero'), may hold values from -0.1875 to 0.1875
- master_out: float32 [4096, 1024], P('zero'), may hold values from -0.09375 to 0.09375
- small_params: float32 [13312], P('zero')
- first_qkv: float32 [1024, 3072], P('zero'), may hold values from -32 to 32
- first_dense: float32 [1024, 1024], P('zero'), may hold values from -12 to 12
- first_in: float32 [1024, 4096], P('zero'), may hold values from -64 to 64
- first_out: float32 [4096, 1024], P('zero'), may hold values from -64 to 64
- first_small: float32 [13312], P('zero'), may hold values from -128 to 128
- second_qkv: float32 [1024, 3072], P('zero'), may hold values from 3.2768 to 26.2144
- second_dense: float32 [1024, 1024], P('zero'), may hold values from 0.32768 to 2.62144
- second_in: float32 [1024, 4096], P('zero'), may hold values from 8.192 to 65.536
- second_out: float32 [4096, 1024], P('zero'), may hold values from 11.79648 to 98.304
- second_small: float32 [13312], P('zero'), may hold values from 32.768 to 262.144
Outputs:
- block_out: bfloat16 [32768, 1024], P(('rep', 'zero', 'ctx'))
- tokens_grad: float32 [32768, 1024], P(('rep', 'zero', 'ctx'))
- grad_qkv: float32 [1024, 3072], P('zero')
- grad_dense: float32 [1024, 1024], P('zero')
- grad_in: float32 [1024, 4096], P('zero')
- grad_out: float32 [4096, 1024], P('zero')
- grad_small: float32 [13312], P('zero')
- renewed_qkv: float32 [1024, 3072], P('zero')
- renewed_dense: float32 [1024, 1024], P('zero')
- renewed_in: float32 [1024, 4096], P('zero')
- renewed_out: float32 [4096, 1024], P('zero')
- renewed_small: float32 [13312], P('zero')
- updated_qkv: float32 [1024, 3072], P('zero')
- updated_dense: float32 [1024, 1024], P('zero')
- updated_in: float32 [1024, 4096], P('zero')
- updated_out: float32 [4096, 1024], P('zero')
- updated_small: float32 [13312], P('zero')
The draws below stay inside these ranges and needn't reach their ends.
Inputs may be any that keep to these rules, and one draw needn't show every extreme that they name: `seq_lengths`: row g gives the lengths of group g's first and second sequence, each at least 1. The second starts at the first multiple of 128 at or after the first's length and ends by 2048. One of the two, first or second, has more than 1792 tokens; the other at most 128. In some group the shorter has 1 token and the longer 2048 - 128.
All inputs are finite; a program needn't handle non-finite values.
Results may differ from the reference program's by a relative error of at most 0.03.
Values may be sent and summed in bfloat16 or wider, within the bound.
A program may use at most 256 MiB of HBM per device.

```python
import math
import jax
import jax.numpy as jnp
from jax import lax

D = 1024
FF = 4096
HEADS = 16
HEAD = 64
ROT = 16
BLOCK = 128
STEP = 10
TOK_DEV = 256
STREAM = 2048
GROUPS = 16
TOKENS = 32768
SMALL = 13312


def draw_seq_lengths(key, part):
    key = jax.random.fold_in(key, 11)
    short_key, long_key, order_key, pick_key = jax.random.split(key, 4)
    chosen = jax.random.randint(pick_key, (), 0, GROUPS, dtype=jnp.int32)
    marked = jnp.arange(GROUPS, dtype=jnp.int32) == chosen
    short_len = jax.random.randint(short_key, (GROUPS,), 1, TOK_DEV - BLOCK + 1, dtype=jnp.int32)
    short_len = jnp.where(marked, 1, short_len)
    short_blocks = (short_len + BLOCK - 1) // BLOCK
    capacity = STREAM - short_blocks * BLOCK
    lowest = STREAM - TOK_DEV + 1
    spread_bits = jax.random.randint(long_key, (GROUPS,), 0, 1 << 20, dtype=jnp.int32)
    long_len = lowest + spread_bits % (capacity - lowest + 1)
    long_len = jnp.where(marked, capacity, long_len)
    order_flag = jax.random.randint(order_key, (GROUPS,), 0, 2, dtype=jnp.int32)
    first_len = jnp.where(order_flag == 1, long_len, short_len)
    second_len = jnp.where(order_flag == 1, short_len, long_len)
    return jnp.stack([first_len, second_len], axis=1).astype(jnp.int32)


def draw_small_params(key, part):
    key = jax.random.fold_in(key, 5)
    jitter = jax.random.normal(key, (SMALL,), jnp.float32)
    offsets = jnp.arange(SMALL)
    is_gain = (offsets < D) | (offsets >= 2 * D) & (offsets < 3 * D)
    return jnp.where(is_gain, 1.0 + 0.1 * jitter, 0.2 * jitter).astype(jnp.float32)


def levels(key, dims, cuts, least, high):
    def one(dim, blocks):
        steps = jax.random.uniform(jax.random.fold_in(jax.random.fold_in(key, 6), dim), (blocks,), jnp.float32, least / len(cuts), high / len(cuts))
        return jnp.repeat(jnp.exp(steps), dims[dim] // blocks).reshape((-1,) + (1,) * (len(dims) - dim - 1))

    level = one(*cuts[0])
    for cut in cuts[1:]:
        level = level * one(*cut)
    return level


def noise(rng, extent, width, limit, shards=(), kind=jnp.bfloat16):
    drawn = width * jax.random.normal(rng, extent, jnp.float32)
    if shards:
        drawn = drawn * levels(rng, extent, shards, -0.22, 0.18)
    return jnp.clip(drawn, -limit, limit).astype(kind)


def setup_inputs(seed: int = 0) -> dict:
    splits = jax.random.split(jax.random.key(seed), 19)
    tokens = noise(splits[0], (TOKENS, D), 1.0, 6.0, ((0, 128),))
    cotangent = noise(splits[1], (TOKENS, D), 1.0, 6.0, ((0, 128),))
    seq_lengths = draw_seq_lengths(jax.random.fold_in(splits[18], 71), 0)
    master_qkv = noise(splits[3], (D, 3 * D), D ** -0.5, 0.1875, ((0, 8),), jnp.float32)
    master_dense = noise(splits[4], (D, D), (D // 64) ** -0.5, 1.5, ((0, 8),), jnp.float32)
    master_in = noise(splits[5], (D, FF), D ** -0.5, 0.1875, ((0, 8),), jnp.float32)
    master_out = noise(splits[6], (FF, D), FF ** -0.5, 0.09375, ((0, 8),), jnp.float32)
    small_params = draw_small_params(jax.random.fold_in(splits[18], 71), 0)
    first_qkv = noise(splits[8], (D, 3 * D), (0.033 * TOKENS ** 0.5), 32.0, ((0, 8),), jnp.float32)
    first_dense = noise(splits[9], (D, D), (0.011 * TOKENS ** 0.5), 12.0, ((0, 8),), jnp.float32)
    first_in = noise(splits[10], (D, FF), (0.055 * TOKENS ** 0.5), 64.0, ((0, 8),), jnp.float32)
    first_out = noise(splits[11], (FF, D), (0.066 * TOKENS ** 0.5), 64.0, ((0, 8),), jnp.float32)
    first_small = noise(splits[12], (SMALL,), (0.11 * TOKENS ** 0.5), 128.0, ((0, 8),), jnp.float32)
    second_qkv = jnp.clip(jnp.exp(math.log(26.2144) - 2.0794415 * jax.random.uniform(splits[13], (D, 3 * D), jnp.float32) ** levels(splits[13], (D, 3 * D), ((0, 8),), -0.2, 0.2)), 3.2768, 26.2144)
    second_dense = jnp.clip(jnp.exp(math.log(2.62144) - 2.0794415 * jax.random.uniform(splits[14], (D, D), jnp.float32) ** levels(splits[14], (D, D), ((0, 8),), -0.2, 0.2)), 0.32768, 2.62144)
    second_in = jnp.clip(jnp.exp(math.log(65.536) - 2.0794415 * jax.random.uniform(splits[15], (D, FF), jnp.float32) ** levels(splits[15], (D, FF), ((0, 8),), -0.2, 0.2)), 8.192, 65.536)
    second_out = jnp.clip(jnp.exp(math.log(98.304) - 2.1202635 * jax.random.uniform(splits[16], (FF, D), jnp.float32) ** levels(splits[16], (FF, D), ((0, 8),), -0.2, 0.2)), 11.79648, 98.304)
    second_small = jnp.clip(jnp.exp(math.log(262.144) - 2.0794415 * jax.random.uniform(splits[17], (SMALL,), jnp.float32) ** levels(splits[17], (SMALL,), ((0, 8),), -0.2, 0.2)), 32.768, 262.144)
    return dict(tokens=tokens, cotangent=cotangent, seq_lengths=seq_lengths, master_qkv=master_qkv, master_dense=master_dense, master_in=master_in, master_out=master_out, small_params=small_params, first_qkv=first_qkv, first_dense=first_dense, first_in=first_in, first_out=first_out, first_small=first_small, second_qkv=second_qkv, second_dense=second_dense, second_in=second_in, second_out=second_out, second_small=second_small)


@jax.custom_vjp
def low(v):
    return lax.optimization_barrier(v.astype(jnp.bfloat16)).astype(jnp.float32)

@jax.custom_vjp
def low_back(v):
    return v

def low_keep(v):
    return (low(v), None)

def low_pass(kept, grad):
    return (grad,)

def back_keep(v):
    return (v, None)

def back_low(kept, grad):
    return (low(grad),)
low.defvjp(low_keep, low_pass)
low_back.defvjp(back_keep, back_low)
PRECISE = lax.Precision.HIGHEST
EPSILON = 1e-05
BETA_ONE = 0.9
BETA_TWO = 0.999
ADAM_EPS = 1e-08
DECAY = 0.01
RATES = (0.25, 1.0, 0.25, 0.2, 0.5)

def layer_norm(values, gain, shift):
    average = lax.optimization_barrier(jnp.mean(values, axis=-1, keepdims=True))
    centered = values - average
    variance = lax.optimization_barrier(jnp.mean(centered * centered, axis=-1, keepdims=True))
    return centered * lax.rsqrt(variance + EPSILON) * gain + shift

def rotate(head_values, position):
    half_rot = ROT // 2
    frequency = 10000.0 ** (-jnp.arange(0, ROT, 2).astype(jnp.float32) / ROT)
    angles = position.astype(jnp.float32)[:, None] * frequency[None, :]
    cosine = jnp.cos(angles)[:, None, :]
    sine_part = jnp.sin(angles)[:, None, :]
    lower_half = head_values[..., :half_rot]
    upper_half = head_values[..., half_rot:ROT]
    return jnp.concatenate([lower_half * cosine - upper_half * sine_part, upper_half * cosine + lower_half * sine_part, head_values[..., ROT:]], axis=-1)

def stream_layout(lengths):
    first_len = lengths[0]
    second_len = lengths[1]
    second_start = (first_len + BLOCK - 1) // BLOCK * BLOCK
    place = jnp.arange(STREAM, dtype=jnp.int32)
    in_first = place < first_len
    in_second = (place >= second_start) & (place < second_start + second_len)
    is_valid = in_first | in_second
    segment = jnp.where(in_first, 0, jnp.where(in_second, 1, 2)).astype(jnp.int32)
    position = jnp.where(in_first, place, jnp.where(in_second, place - second_start, 0)).astype(jnp.int32)
    return (segment, position, is_valid)

def group_forward(params, inputs, segment, position, is_valid):
    master_qkv, master_dense, master_in, master_out, small_params = params
    small_vals = low(small_params)
    gain_attn = small_vals[0:D]
    shift_attn = small_vals[D:2 * D]
    gain_mlp = small_vals[2 * D:3 * D]
    shift_mlp = small_vals[3 * D:4 * D]
    bias_qkv = small_vals[4 * D:7 * D]
    bias_dense = small_vals[7 * D:8 * D]
    bias_out = small_vals[8 * D:9 * D]
    bias_in = small_vals[9 * D:9 * D + FF]
    normed_attn = low(layer_norm(inputs, gain_attn, shift_attn))
    projected = low_back(jnp.dot(normed_attn, low(master_qkv), precision=PRECISE) + bias_qkv)
    query_rows = low(rotate(projected[:, :D].reshape(STREAM, HEADS, HEAD), position))
    key_rows = low(rotate(projected[:, D:2 * D].reshape(STREAM, HEADS, HEAD), position))
    values = low(projected[:, 2 * D:].reshape(STREAM, HEADS, HEAD))
    key_index = jnp.arange(STREAM, dtype=jnp.int32)
    block_rows = min(512, STREAM)
    starts = jnp.arange(STREAM // block_rows, dtype=jnp.int32) * block_rows

    def attend(block_start):
        query_block = lax.dynamic_slice_in_dim(query_rows, block_start, block_rows, 0)
        query_index = block_start + jnp.arange(block_rows, dtype=jnp.int32)
        seg_block = lax.dynamic_slice_in_dim(segment, block_start, block_rows, 0)
        valid_block = lax.dynamic_slice_in_dim(is_valid, block_start, block_rows, 0)
        visible = (seg_block[:, None] == segment[None, :]) & valid_block[:, None] & is_valid[None, :] & (key_index[None, :] <= query_index[:, None]) | (key_index[None, :] == query_index[:, None])
        scores = low_back(jnp.einsum('qhd,khd->hqk', query_block, key_rows, precision=PRECISE) * 0.125)
        scores = jnp.where(visible[None], scores, -1e+30)
        row_top = lax.optimization_barrier(jnp.max(scores, axis=-1, keepdims=True))
        weights = jnp.exp(scores - row_top)
        attn_probs = weights / lax.optimization_barrier(jnp.sum(weights, axis=-1, keepdims=True))
        return jnp.einsum('hqk,khd->qhd', low(attn_probs), values, precision=PRECISE)
    attended = lax.map(jax.checkpoint(attend), starts).reshape(STREAM, D)
    attended = low(low_back(attended))
    attention = jnp.dot(attended, low(master_dense), precision=PRECISE) + bias_dense
    normed_mlp = low(layer_norm(inputs, gain_mlp, shift_mlp))
    hidden = low_back(jnp.dot(normed_mlp, low(master_in), precision=PRECISE) + bias_in)
    act_low = low(jax.nn.gelu(hidden, approximate=False))
    mlp = jnp.dot(act_low, low(master_out), precision=PRECISE) + bias_out
    return inputs + attention + mlp

def add_trees(left_tree, right_tree):
    return jax.tree.map(jnp.add, left_tree, right_tree)

def adam_update(master, first_old, second_old, gradient, step_rate):
    first_new = BETA_ONE * first_old + (1.0 - BETA_ONE) * gradient
    second_new = BETA_TWO * second_old + (1.0 - BETA_TWO) * gradient * gradient
    first_hat = first_new / (1.0 - BETA_ONE ** STEP)
    second_hat = second_new / (1.0 - BETA_TWO ** STEP)
    updated = master - step_rate * (first_hat / (jnp.sqrt(second_hat) + ADAM_EPS) + DECAY * master)
    return (gradient, second_new, updated)

def reference(tokens, cotangent, seq_lengths, master_qkv, master_dense, master_in, master_out, small_params, first_qkv, first_dense, first_in, first_out, first_small, second_qkv, second_dense, second_in, second_out, second_small):
    params = (master_qkv, master_dense, master_in, master_out, small_params)
    token_groups = tokens.astype(jnp.float32).reshape(GROUPS, STREAM, D)
    back_groups = cotangent.astype(jnp.float32).reshape(GROUPS, STREAM, D)

    def one_group(totals, entry):
        group_tokens, group_back, lengths = entry
        segment, position, is_valid = stream_layout(lengths)

        def forward(param_tree, inputs):
            return group_forward(param_tree, inputs, segment, position, is_valid)
        outputs, pullback = jax.vjp(forward, params, group_tokens)
        masked_back = group_back * is_valid[:, None].astype(jnp.float32)
        param_grads, token_grad = pullback(masked_back)
        return (add_trees(totals, param_grads), (outputs.astype(jnp.bfloat16), token_grad))
    zero_tree = jax.tree.map(jnp.zeros_like, params)
    gradients, (outputs, token_grads) = lax.scan(one_group, zero_tree, (token_groups, back_groups, seq_lengths))
    firsts = (first_qkv, first_dense, first_in, first_out, first_small)
    seconds = (second_qkv, second_dense, second_in, second_out, second_small)
    results = [adam_update(params[item], firsts[item], seconds[item], gradients[item], RATES[item]) for item in range(5)]
    return (outputs.reshape(TOKENS, D), token_grads.reshape(TOKENS, D), results[0][0], results[1][0], results[2][0], results[3][0], results[4][0], results[0][1], results[1][1], results[2][1], results[3][1], results[4][1], results[0][2], results[1][2], results[2][2], results[3][2], results[4][2])
```

```python
import functools
import math

import jax
import jax.numpy as jnp
from jax import lax
from jax.experimental import pallas as pl
from jax.experimental.pallas import tpu as pltpu
from jax.sharding import PartitionSpec as P

D = 1024
T = 2048
R = 256
NB = 8
BLOCK = 128
STEP = 10
QKV = 384
UP = 512
WIDE = QKV + UP
DOWN = 640
EPSILON = 1e-05
BETA_ONE = 0.9
BETA_TWO = 0.999
ADAM_EPS = 1e-08
DECAY = 0.01
RATES = (0.25, 1.0, 0.25, 0.2, 0.5)
NEG = -1e30
BF = jnp.bfloat16
F32 = jnp.float32
MESH = pl.DeviceIdType.MESH


def nn(a, b):
    return lax.dot_general(a, b, (((1,), (0,)), ((), ())), preferred_element_type=F32)


def nt(a, b):
    return lax.dot_general(a, b, (((1,), (1,)), ((), ())), preferred_element_type=F32)


def rows(block):
    return pl.ds(pl.multiple_of(block * R, R), R)


def part(index, size):
    return pl.ds(pl.multiple_of(index * size, size), size)


def turns(table):
    lane = lax.broadcasted_iota(jnp.int32, table.shape, 1) % 64
    return jnp.where(lane < 16, table, 1.0), jnp.where(lane < 16, pltpu.roll(table, 112, 1), 0.0)


def rope(u, cosine, sine, sign):
    lane = lax.broadcasted_iota(jnp.int32, u.shape, 1) % 64
    above = pltpu.roll(u, 8, 1)
    below = pltpu.roll(u, u.shape[1] - 8, 1)
    return u * cosine + (sign * jnp.where(lane < 8, -below, above)) * sine


def head_mask(x, head):
    lane = lax.broadcasted_iota(jnp.int32, x.shape, 1)
    return jnp.where((lane >= 64 * head) & (lane < 64 * head + 64), x, jnp.zeros_like(x))


def visible(i, j, low):
    key = lax.broadcasted_iota(jnp.int32, (R, R), 0) + j * R
    query = lax.broadcasted_iota(jnp.int32, (R, R), 1) + i * R
    return (key >= low) & (key <= query)


def project(b, s):
    nb = s.n[rows(b), :]
    s.nT[:, rows(b)] = nb.T
    h = nn(nb, s.w1[:, :QKV]) + s.bias[0:1, :QKV]
    cosine, sine = turns(s.turn[rows(b), :])
    s.q[rows(b), :] = (rope(h[:, :128], cosine, sine, 1.0) * 0.125).astype(BF)
    kb = rope(h[:, 128:256], cosine, sine, 1.0).astype(BF)
    vb = h[:, 256:384].astype(BF)
    s.k[rows(b), :] = kb
    s.kT[:, rows(b)] = kb.T
    s.v[rows(b), :] = vb
    s.vT[:, rows(b)] = vb.T
    for t in range(2):
        cols = slice(QKV + 256 * t, QKV + 256 * t + 256)
        hid = slice(128 + 256 * t, 384 + 256 * t)
        x = nn(nb, s.w1[:, cols]) + s.bias[0:1, cols]
        cdf = 0.5 + 0.5 * lax.erf(x * (1 / math.sqrt(2)))
        pdf = jnp.exp(-0.5 * x * x) * (1 / math.sqrt(2 * math.pi))
        act = (x * cdf).astype(BF)
        s.dP[rows(b), cols] = (cdf + x * pdf).astype(BF)
        s.A[rows(b), hid] = act
        s.AT[hid, rows(b)] = act.T


def attend(i, s):
    qb = s.q[rows(i), :]
    low = s.low[0:1, rows(i)]
    heads = [head_mask(qb, h) for h in range(2)]

    def block(j, carry):
        out = []
        kb = s.k[rows(j), :]
        seen = visible(i, j, low)
        for h in range(2):
            top, total, o = carry[3 * h : 3 * h + 3]
            scores = jnp.where(seen, nt(kb, heads[h]), NEG)
            new = jnp.maximum(top, jnp.max(scores, axis=0, keepdims=True))
            p = jnp.exp(scores - new)
            scale = jnp.exp(top - new)
            total = total * scale + jnp.sum(p, axis=0, keepdims=True)
            o = o * scale + nn(s.vT[64 * h : 64 * h + 64, rows(j)], p.astype(BF))
            out += [new, total, o]
        return tuple(out)

    start = (jnp.full((1, R), NEG, F32), jnp.zeros((1, R), F32), jnp.zeros((64, R), F32)) * 2
    carry = lax.fori_loop(0, i, block, block(i, start))
    oT = jnp.concatenate([carry[2] / carry[1], carry[5] / carry[4]], axis=0).astype(BF)
    s.AT[0:128, rows(i)] = oT
    s.A[rows(i), 0:128] = oT.T
    for h in range(2):
        s.lse[h : h + 1, rows(i)] = carry[3 * h] + jnp.log(carry[3 * h + 1])


def pull_down(b, s):
    bb = s.back[rows(b), :]
    s.dO[rows(b), :] = nt(bb, s.w2[0:128, :]).astype(BF)
    for t in range(2):
        cols = slice(QKV + 256 * t, QKV + 256 * t + 256)
        d = nt(bb, s.w2[128 + 256 * t : 384 + 256 * t, :])
        s.dP[rows(b), cols] = (d * s.dP[rows(b), cols].astype(F32)).astype(BF)


def attend_back(i, s):
    qb, db = s.q[rows(i), :], s.dO[rows(i), :]
    low = s.low[0:1, rows(i)]
    qh = [head_mask(qb, h) for h in range(2)]
    dh = [head_mask(db, h) for h in range(2)]
    w = db.astype(F32).T * s.AT[0:128, rows(i)].astype(F32)
    delta = [jnp.sum(w[64 * h : 64 * h + 64], axis=0, keepdims=True) for h in range(2)]
    lse = [s.lse[h : h + 1, rows(i)] for h in range(2)]

    def block(j, dq):
        kb, vb = s.k[rows(j), :], s.v[rows(j), :]
        seen = visible(i, j, low)
        new, dk, dv = [], 0.0, 0.0
        for h in range(2):
            p = jnp.where(seen, jnp.exp(nt(kb, qh[h]) - lse[h]), 0.0)
            ds = (p * (nt(vb, dh[h]) - delta[h])).astype(BF)
            dv = dv + nn(p.astype(BF), dh[h])
            dk = dk + nn(ds, qh[h])
            new.append(dq[h] + nn(s.kT[64 * h : 64 * h + 64, rows(j)], ds))
        s.dv[rows(j), :] += dv
        s.dk[rows(j), :] += dk
        return tuple(new)

    zero = jnp.zeros((64, R), F32)
    dq = lax.fori_loop(0, i + 1, block, (zero, zero))
    cosine, sine = turns(s.turn[rows(i), :])
    dqT = jnp.concatenate(dq, axis=0) * 0.125
    s.dP[rows(i), 0:128] = rope(dqT.T, cosine, sine, -1.0).astype(BF)
    s.dP[rows(i), 128:256] = rope(s.dk[rows(i), :], cosine, sine, -1.0).astype(BF)
    s.dP[rows(i), 256:384] = s.dv[rows(i), :].astype(BF)
    s.back[rows(i), :] = nt(s.dP[rows(i), :], s.w1[...]).astype(BF)


def unit_norm(x):
    mean = jnp.mean(x, axis=-1, keepdims=True)
    centered = x - mean
    var = jnp.mean(centered * centered, axis=-1, keepdims=True)
    inv = lax.rsqrt(var + EPSILON)
    return centered * inv, inv


VMEM_SHAPES = dict(
    n=((T, D), BF), nT=((D, T), BF), back=((T, D), BF),
    w1r=((D, WIDE), BF), w1=((D, WIDE), BF), w2=((DOWN, D), BF),
    q=((T, 128), BF), k=((T, 128), BF), v=((T, 128), BF), kT=((128, T), BF), vT=((128, T), BF),
    A=((T, DOWN), BF), AT=((DOWN, T), BF), dP=((T, WIDE), BF), dO=((T, 128), BF),
    dk=((T, 128), F32), dv=((T, 128), F32), lse=((8, T), F32), low=((8, T), jnp.int32),
    angle=((16, T), F32), turn=((T, 128), F32),
    bias=((8, WIDE), F32), flat=((104, 128), F32), cols=((128, 32), F32),
    sibO=((4, R, D), BF), xO=((3, R, D), BF), sibE=((4, R, D), BF), xE=((3, R, D), BF),
    small=((8, 16, 128), F32), flatG=((104, 128), F32), smallG=((2, 4, 16, 128), F32), smallZ=((3, 4, 16, 128), F32),
    smallT=((4, 16, 128), F32), smallY=((3, 16, 128), F32), smallU=((16, 128), F32), smallX=((3, 16, 128), F32),
    smallV=((16, 128), F32), smallS=((16, 128), F32),
    gi=((4, 4, 64, UP), BF), gq=((4, 4, 64, QKV), BF), gd=((2, 64, D), BF), go=((4, 2, 64, D), BF),
    zi=((3, 4, 64, UP), BF), zq=((3, 4, 64, QKV), BF), zd=((3, 64, D), BF), yo=((3, 2, 64, D), BF),
    ti=((4, 64, UP), BF), tq=((4, 64, QKV), BF), td=((64, D), BF), to=((2, 64, D), BF),
    yi=((3, 64, UP), BF), yq=((3, 64, QKV), BF), yd=((3, 64, D), BF), zo=((3, 64, D), BF),
    fi=((2, 64, UP), BF), fq=((2, 64, QKV), BF), fd=((2, 64, D), BF), fo=((2, 64, D), BF),
)
SEMS = dict(
    load=23, n=10, back=10, w1=11, wo=11, wd=11, small=7,
    sibO=4, xO=3, sibE=4, xE=3, zi=3, zq=3, zd=3, yo=3, yi=3, yq=3, yd=3, zo=3,
    smallZ=3, smallY=3, smallX=3, smallS=1,
    ri=1, rq=1, rd=1, ro=1, ai=8, aq=8, ao=8, ad=8,
)


class Holder:
    pass


class Transfer:
    def __init__(self, copy, send_if=None, recv_if=None):
        self.copy, self.send_if, self.recv_if = copy, send_if, recv_if

    def only(self, condition, act):
        if condition is None:
            act()
        else:
            pl.when(condition)(act)

    def start(self):
        self.only(self.send_if, self.copy.start)

    def wait_send(self):
        self.only(self.send_if, self.copy.wait_send)

    def wait_recv(self):
        self.only(self.recv_if, self.copy.wait_recv)


def each(f, lo=0, hi=NB):
    def body(i, carry):
        f(i)
        return carry

    lax.fori_loop(lo, hi, body, 0)


def kernel(
    tokens, cot, lens, small_in, m_qkv, m_dense, m_in, m_out,
    block_out, tokens_grad, o_qkv, o_in, o_out, o_dense, o_small, *scratch,
):
    s = Holder()
    it = iter(scratch)
    for name in VMEM_SHAPES:
        setattr(s, name, next(it))
    sends = {name: next(it) for name in SEMS}
    recvs = {name: next(it) for name in SEMS}

    r, z, c = lax.axis_index("rep"), lax.axis_index("zero"), lax.axis_index("ctx")
    y, zl, x, core = z // 2, lax.rem(z, 2), c // 2, lax.rem(c, 2)

    def dev(rr, yy, ll, xx, kk):
        return (rr, yy * 2 + ll, xx * 2 + kk)

    def make(name, index, src, dst, target, send_if=None, recv_if=None):
        copy = pltpu.make_async_remote_copy(
            src_ref=src, dst_ref=dst, send_sem=sends[name].at[index], recv_sem=recvs[name].at[index],
            device_id=target, device_id_type=MESH)
        return Transfer(copy, send_if, recv_if)

    def start(transfers):
        for transfer in transfers:
            transfer.start()
        return transfers

    def wait_recv(transfers):
        for transfer in transfers:
            transfer.wait_recv()

    def wait_send(transfers):
        for transfer in transfers:
            transfer.wait_send()

    def y_at(d):
        return lax.rem(y + d, 4)

    def x_at(d):
        return lax.rem(x + d, 4)

    def z_at(d):
        place = lax.rem(2 * r + zl + d, 4)
        return place // 2, lax.rem(place, 2)

    def along_x(d):
        return dev(r, y, zl, x_at(d), core)

    def along_y(d):
        return dev(r, y_at(d), zl, x, core)

    def along_z(d):
        rr, ll = z_at(d)
        return dev(rr, y, ll, x, core)

    def block_of(xx, kk):
        return xx * 2 + kk

    sib = dev(r, y, zl, x, 1 - core)
    diagonal = z == c
    plane = zl == core
    finals = []

    loads = []

    def load(index, src, dst):
        copy = pltpu.make_async_copy(src, dst, sends["load"].at[index])
        copy.start()
        loads.append(copy)

    for t in range(3):
        load(t, m_qkv.at[:, part(c + 8 * t, 128)], s.dk.at[128 * t : 128 * t + 128, :])
    for t in range(3, 7):
        load(t, m_in.at[:, part((2 * (t - 3) + core) * 4 + x, 128)], s.dk.at[128 * t : 128 * t + 128, :])
    for t in range(8):
        load(7 + t, m_out.at[part(x, 128), 128 * t : 128 * t + 128], s.dv.at[128 * t : 128 * t + 128, :])
        load(15 + t, m_dense.at[:, 128 * t : 128 * t + 128], s.dv.at[D + 128 * t : D + 128 * t + 128, :])

    barrier = pltpu.get_barrier_semaphore()
    peers = [along_x(1), along_x(2), along_x(3), sib]
    for dr in range(2):
        for dy in range(4):
            for dl in range(2):
                if dr or dy or dl:
                    peers.append(dev(lax.rem(r + dr, 2), y_at(dy), lax.rem(zl + dl, 2), x, core))
    for p in peers:
        pl.semaphore_signal(barrier, inc=1, device_id=p, device_id_type=MESH)

    own, inverse = unit_norm(tokens[...].astype(F32))
    s.n[rows(c), :] = own.astype(BF)
    first, second = lens[0, 0], lens[0, 1]
    second_start = (first + BLOCK - 1) // BLOCK * BLOCK

    def masked_cotangent():
        place = lax.broadcasted_iota(jnp.int32, (R, D), 0) + c * R
        valid = (place < first) | ((place >= second_start) & (place < second_start + second))
        return jnp.where(valid, cot[...].astype(F32), 0.0)

    s.back[rows(c), :] = masked_cotangent().astype(BF)
    s.small[pl.ds(z, 1)] = small_in[...].astype(BF).astype(F32)[None]
    for t in range(7):
        loads[t].wait()
        s.w1r[part(z, 128), 128 * t : 128 * t + 128] = s.dk[128 * t : 128 * t + 128, :].astype(BF)
    pl.semaphore_wait(barrier, len(peers))

    lb, rb, ob = block_of(x_at(3), core), block_of(x_at(1), core), block_of(x_at(2), core)

    def gather(name, buf):
        def half(b, h):
            return buf.at[pl.ds(pl.multiple_of(b * R + 128 * h, 128), 128), :]

        def whole(b):
            return buf.at[rows(b), :]

        def same(index, ref, target):
            return make(name, index, ref, ref, target)

        return [
            same(0, half(c, 0), along_x(1)),
            same(1, half(c, 1), along_x(3)),
            same(2, half(c, 1), along_x(1)),
            same(3, half(c, 0), along_x(3)),
            same(4, whole(c), sib),
            same(5, half(lb, 0), along_x(1)),
            same(6, half(rb, 1), along_x(3)),
            same(7, whole(lb), sib),
            same(8, whole(rb), sib),
            same(9, whole(ob), sib),
        ]

    def gather_forward(g):
        for got, sent in ((0, 5), (1, 6), (2, 7), (3, 8)):
            g[got].wait_recv()
            g[sent].start()

    def gather_across(g):
        g[5].wait_recv()
        g[6].wait_recv()
        g[9].start()

    def gather_done(g):
        wait_recv([g[4], g[7], g[8], g[9]])

    n_gather = gather("n", s.n)
    start(n_gather[:5])

    def spread(name, buf, row, same_send=None, same_recv=None, cross_send=None, cross_recv=None):
        out = []
        whole = buf.at[pl.ds(pl.multiple_of(row, 128), 128), :]
        for dy in (1, 3, 2):
            recv_if = same_recv(dy) if same_recv else None
            out.append(make(name, dy - 1, whole, whole, along_y(dy), same_send, recv_if))
        for dy in (0, 1, 3, 2):
            for h in range(2):
                ref = buf.at[pl.ds(pl.multiple_of(row + 64 * h, 64), 64), :]
                target = dev(r if h == 0 else 1 - r, y_at(dy), 1 - zl, x, core)
                recv_if = cross_recv(dy) if cross_recv else None
                out.append(make(name, 3 + 2 * dy + h, ref, ref, target, cross_send, recv_if))
        return out

    small_gather = []
    for dy in range(4):
        for dl in range(2):
            if dy or dl:
                target = dev(r, y_at(dy), lax.rem(zl + dl, 2), x, core)
                small_gather.append(make("small", 2 * dy + dl - 1, s.small.at[z], s.small.at[z], target))
    start(small_gather)
    w1_spread = spread("w1", s.w1r, z * 128)
    start(w1_spread)

    lane_place = lax.broadcasted_iota(jnp.int32, (8, T), 1)
    in_first = lane_place < first
    in_second = (lane_place >= second_start) & (lane_place < second_start + second)
    s.low[...] = jnp.where(in_first, 0, jnp.where(in_second, second_start, lane_place))
    position = jnp.where(in_first, lane_place, jnp.where(in_second, lane_place - second_start, 0))
    entry = lax.broadcasted_iota(jnp.int32, (8, T), 0)
    frequency = jnp.zeros((8, T), F32)
    for t in range(8):
        frequency = jnp.where(entry == t, 10000.0 ** (-t / 8), frequency)
    turn = position.astype(F32) * frequency
    s.angle[0:8, :] = jnp.cos(turn)
    s.angle[8:16, :] = jnp.sin(turn)

    def tables(b):
        cs, sn = s.angle[0:8, rows(b)], s.angle[8:16, rows(b)]
        rest = jnp.zeros((32, R), F32)
        s.turn[rows(b), :] = jnp.concatenate([cs, cs, sn, sn, rest] * 2, axis=0).T

    each(tables)
    s.flatG[...] = jnp.zeros_like(s.flatG)
    s.smallG[...] = jnp.zeros_like(s.smallG)

    gather_forward(n_gather)
    back_gather = gather("back", s.back)
    start(back_gather[:5])

    for t in range(7, 23):
        loads[t].wait()
    wo_row = 128 + y * 128
    wo_spread = spread("wo", s.w2, wo_row, plane, lambda dy: plane, plane, lambda dy: zl != core)

    def dense_from(dy):
        return lax.rem(y + 4 - dy, 4) == x

    wd_spread = spread(
        "wd", s.w2, 0, diagonal, lambda dy: dense_from(dy) & plane, diagonal, lambda dy: dense_from(dy) & (zl != core))

    @pl.when(plane)
    def _():
        for t in range(8):
            cols = slice(128 * t, 128 * t + 128)
            s.w2[pl.ds(pl.multiple_of(wo_row, 128), 128), cols] = s.dv[128 * t : 128 * t + 128, :].astype(BF)

    @pl.when(diagonal)
    def _():
        for t in range(8):
            s.w2[0:128, 128 * t : 128 * t + 128] = s.dv[D + 128 * t : D + 128 * t + 128, :].astype(BF)

    s.dk[...] = jnp.zeros_like(s.dk)
    s.dv[...] = jnp.zeros_like(s.dv)
    start(wd_spread)
    start(wo_spread)

    wait_recv(small_gather)
    for t in range(8):
        s.flat[13 * t : 13 * t + 13, :] = s.small[t, 0:13, :]
    s.cols[...] = s.flat[0:32, :].T
    wait_recv(w1_spread)

    def line(at):
        return jnp.concatenate([s.flat[at + t : at + t + 1, :] for t in range(8)], axis=1)

    shifts = jnp.concatenate([line(8), line(24), jnp.zeros((6, D), F32)], axis=0).astype(BF)
    turned = nn(shifts, s.w1r[...])
    for t in range(3):
        cols = slice(128 * t, 128 * t + 128)
        s.bias[0:1, cols] = turned[0:1, cols] + s.flat[pl.ds(32 + 8 * t + c, 1), :]
    for t in range(4):
        cols = slice(QKV + 128 * t, QKV + 128 * t + 128)
        s.bias[0:1, cols] = turned[1:2, cols] + s.flat[pl.ds(72 + (2 * t + core) * 4 + x, 1), :]
    for t in range(8):
        sl = slice(128 * t, 128 * t + 128)
        s.w1[sl, :QKV] = (s.w1r[sl, :QKV].astype(F32) * s.cols[:, t : t + 1]).astype(BF)
        s.w1[sl, QKV:] = (s.w1r[sl, QKV:].astype(F32) * s.cols[:, 16 + t : 17 + t]).astype(BF)

    gather_across(n_gather)
    gather_done(n_gather)
    each(lambda b: project(b, s))
    gather_forward(back_gather)
    each(lambda i: attend(i, s), 0, 6)
    gather_across(back_gather)
    each(lambda i: attend(i, s), 6, 8)

    def to_sibling(name, buf, slots, xx):
        return make(name, xx, buf.at[rows(block_of(xx, 1 - core)), :], slots.at[xx], sib)

    def to_owner(name, buf, slots, xx, d):
        return make(name, d - 1, buf.at[rows(block_of(xx, core)), :], slots.at[d - 1], dev(r, y, zl, xx, core))

    def owner_sum(name, buf, slots, name_x, slots_x, xx):
        to_sibling(name, buf, slots, xx).wait_recv()
        mine = buf[rows(block_of(xx, core)), :].astype(F32) + slots[pl.ds(xx, 1)][0].astype(F32)
        buf[rows(block_of(xx, core)), :] = mine.astype(BF)

        @pl.when(xx != x)
        def _():
            to_owner(name_x, buf, slots_x, xx, lax.rem(x + 4 - xx, 4)).start()

    def owner_total(name_x, buf, slots_x):
        total = buf[rows(c), :].astype(F32)
        for d in (1, 3, 2):
            to_owner(name_x, buf, slots_x, x_at(4 - d), d).wait_recv()
            total = total + slots_x[d - 1].astype(F32)
        return total

    def owner_drain(name, buf, slots, name_x, slots_x):
        for xx in range(4):
            to_sibling(name, buf, slots, xx).wait_send()
        for d in (1, 2, 3):
            to_owner(name_x, buf, slots_x, x_at(4 - d), d).wait_send()

    def down(i):
        s.n[rows(i), :] = nn(s.A[rows(i), :], s.w2[...]).astype(BF)

    def down_first(xx):
        down(block_of(xx, 1 - core))
        to_sibling("sibO", s.n, s.sibO, xx).start()

    wait_recv(wd_spread)
    wait_recv(wo_spread)
    wait_send(n_gather)
    each(down_first, 0, 4)
    each(lambda xx: down(block_of(xx, core)), 0, 4)
    gather_done(back_gather)
    each(lambda b: pull_down(b, s))
    each(lambda xx: owner_sum("sibO", s.n, s.sibO, "xO", s.xO, xx), 0, 4)

    def grad_down(t):
        cols = part(t, 256)
        g = nn(s.AT[...], s.back[:, cols]).astype(BF)
        for h in range(2):
            s.gd[h, :, cols] = g[64 * h : 64 * h + 64]
            for yy in range(4):
                s.go[yy, h, :, cols] = g[128 + 128 * yy + 64 * h : 192 + 128 * yy + 64 * h]

    each(grad_down, 0, 4)

    def down_grads_out():
        out = [make("yo", d - 1, s.go.at[y_at(d)], s.yo.at[d - 1], along_y(d)) for d in (1, 3, 2)]
        for d in (1, 3, 2):
            rr, ll = z_at(d)
            out.append(make("zd", d - 1, s.gd.at[rr], s.zd.at[d - 1], along_z(d), ll == core, plane))
        return out

    down_sends = start(down_grads_out())

    def grad_up(lo, hi, out, at, gain_at, shift_at):
        g = nn(s.nT[...], s.dP[:, lo:hi])
        total = jnp.sum(s.dP[:, lo:hi].astype(F32), axis=0, keepdims=True)
        gains, moves = [], []
        for t in range(8):
            sl = slice(128 * t, 128 * t + 128)
            w = s.w1r[sl, lo:hi].astype(F32)
            gains.append(jnp.sum(w * g[sl], axis=1, keepdims=True))
            moves.append(jnp.sum(w * total, axis=1, keepdims=True))
            full = g[sl] * s.cols[:, gain_at + t : gain_at + t + 1] + s.cols[:, shift_at + t : shift_at + t + 1] * total
            for h in range(2):
                out[2 * h + t % 2, t // 2, :, at : at + hi - lo] = full[64 * h : 64 * h + 64].astype(BF)
        return total, jnp.concatenate(gains, axis=1), jnp.concatenate(moves, axis=1)

    total_a, gain_a, move_a = grad_up(QKV, QKV + 256, s.gi, 0, 16, 24)
    total_b, gain_b, move_b = grad_up(QKV + 256, WIDE, s.gi, 256, 16, 24)
    s.flatG[16:32, :] = jnp.concatenate([gain_a + gain_b, move_a + move_b], axis=1).T
    for t in range(4):
        total = total_a if t < 2 else total_b
        at = 128 * (t % 2)
        s.flatG[pl.ds(72 + (2 * t + core) * 4 + x, 1), :] = total[:, at : at + 128]
    back_sum = jnp.sum(s.back[rows(c), :].astype(F32), axis=0, keepdims=True)
    for t in range(8):
        s.flatG[56 + t : 57 + t, :] = back_sum[:, 128 * t : 128 * t + 128]
        s.flatG[64 + t : 65 + t, :] = back_sum[:, 128 * t : 128 * t + 128]

    def z_sends(name, src, slots):
        return [make(name, d - 1, src.at[2 * z_at(d)[0] + z_at(d)[1]], slots.at[d - 1], along_z(d)) for d in (1, 3, 2)]

    def y_sends(name, src, slots):
        return [make(name, d - 1, src.at[y_at(d)], slots.at[d - 1], along_y(d)) for d in (1, 3, 2)]

    def z_sum(transfers, src, slots, out):
        wait_recv(transfers)
        mine = src[pl.ds(2 * r + zl, 1)][0].astype(F32)
        for d in range(3):
            mine = mine + slots[d].astype(F32)
        out[...] = mine.astype(out.dtype)

    def y_sum(transfers, src, slots):
        wait_recv(transfers)
        mine = src[pl.ds(y, 1)][0].astype(F32)
        for d in range(3):
            mine = mine + slots[d].astype(F32)
        return mine

    zi_sends = start(z_sends("zi", s.gi, s.zi))
    wait_send(back_gather)

    def back_pair(p):
        xx = 3 - p

        def one(h):
            attend_back(block_of(xx, 1 - h), s)

        each(one, 0, 2)
        to_sibling("sibE", s.back, s.sibE, xx).start()

        @pl.when(p > 0)
        def _():
            owner_sum("sibE", s.back, s.sibE, "xE", s.xE, xx + 1)

    each(back_pair, 0, 2)

    yi_sends = y_sends("yi", s.ti, s.yi)
    z_sum(zi_sends, s.gi, s.zi, s.ti)
    start(yi_sends)
    wait_recv(down_sends)
    s.to[...] = (
        s.go[pl.ds(y, 1)][0].astype(F32) + s.yo[0].astype(F32) + s.yo[1].astype(F32) + s.yo[2].astype(F32)).astype(BF)
    second_sends = []
    for d in (1, 3, 2):
        rr, ll = z_at(d)
        second_sends.append(make("zo", d - 1, s.to.at[rr], s.zo.at[d - 1], along_z(d), ll == core, plane))

    def to_diagonal(d):
        return make("yd", d - 1, s.td, s.yd.at[d - 1], along_y(d), plane & (y_at(d) == x), diagonal)

    second_dense = [to_diagonal(d) for d in (1, 3, 2)]

    @pl.when(plane)
    def _():
        mine = s.gd[pl.ds(r, 1)][0].astype(F32)
        for d in range(3):
            mine = mine + s.zd[d].astype(F32)
        s.td[...] = mine.astype(BF)

    start(second_sends)
    start(second_dense)

    each(back_pair, 2, 3)

    other = dev(1 - r, y, zl, x, core)

    def halves(name, buf, condition=None):
        return make(name, 0, buf.at[r], buf.at[r], other, condition, condition)

    s.fi[pl.ds(r, 1)] = y_sum(yi_sends, s.ti, s.yi).astype(BF)[None]
    wait_recv(second_sends)
    wait_recv(second_dense)

    @pl.when(plane)
    def _():
        mine = s.to[pl.ds(r, 1)][0].astype(F32)
        for d in range(3):
            mine = mine + s.zo[d].astype(F32)
        s.fo[pl.ds(r, 1)] = mine.astype(BF)[None]

    @pl.when(diagonal)
    def _():
        mine = s.td[...].astype(F32)
        for d in range(3):
            mine = mine + s.yd[d].astype(F32)
        s.fd[pl.ds(r, 1)] = mine.astype(BF)[None]

    early = start([halves("ri", s.fi), halves("ro", s.fo, plane), halves("rd", s.fd, diagonal)])

    each(back_pair, 3, 4)
    owner_sum("sibE", s.back, s.sibE, "xE", s.xE, 0)

    total_q, gain_q, move_q = grad_up(0, 256, s.gq, 0, 0, 8)
    total_v, gain_v, move_v = grad_up(256, QKV, s.gq, 256, 0, 8)
    zq_sends = start(z_sends("zq", s.gq, s.zq))
    s.flatG[0:16, :] = jnp.concatenate([gain_q + gain_v, move_q + move_v], axis=1).T
    s.flatG[pl.ds(32 + c, 1), :] = total_q[:, 0:128]
    s.flatG[pl.ds(40 + c, 1), :] = total_q[:, 128:256]
    s.flatG[pl.ds(48 + c, 1), :] = total_v
    for t in range(8):
        s.smallG[t % 2, t // 2, 0:13, :] = s.flatG[13 * t : 13 * t + 13, :]
    small_z = start([make("smallZ", d - 1, s.smallG.at[z_at(d)[1]], s.smallZ.at[d - 1], along_z(d)) for d in (1, 3, 2)])

    def final_gather(name, buf, out, slot, source=None):
        def has(xx, kk):
            return source(xx, kk) if source else None

        def at(xx, kk):
            return slot(out, xx, kk)

        local = pltpu.make_async_copy(buf, at(x, core), sends[name].at[7])
        first_hop = [
            make(name, d - 1, buf, at(x, core), along_x(d), has(x, core), has(x_at(4 - d), core)) for d in (1, 3, 2)]
        first_hop.append(make(name, 3, buf, at(x, core), sib, has(x, core), has(x, 1 - core)))
        second_hop = []
        for d in (1, 3, 2):
            xx = x_at(4 - d)
            ref = at(xx, core)
            second_hop.append(make(name, 3 + d, ref, ref, sib, has(xx, core), has(xx, 1 - core)))
        own_copy = Transfer(local, has(x, core))
        own_copy.start()
        start(first_hop)
        return own_copy, first_hop, second_hop

    def final_forward(g):
        own_copy, first_hop, second_hop = g
        for got, sent in zip(first_hop[:3], second_hop):
            got.wait_recv()
            sent.start()

    def final_finish(g):
        own_copy, first_hop, second_hop = g
        own_copy.only(own_copy.send_if, own_copy.copy.wait)
        first_hop[3].wait_recv()
        wait_recv(second_hop)
        finals.extend(first_hop + second_hop)

    wait_recv(early)
    by_ctx = lambda out, xx, kk: out.at[block_of(xx, kk)]
    g_in = final_gather("ai", s.fi, o_in, by_ctx)
    g_out = final_gather("ao", s.fo, o_out, lambda out, xx, kk: out.at[xx], lambda xx, kk: zl == kk)
    g_dense = final_gather("ad", s.fd, o_dense, lambda out, xx, kk: out, lambda xx, kk: (zl == kk) & (y == xx))

    total = owner_total("xO", s.n, s.xO)
    bias = jnp.concatenate([s.flat[56 + t : 57 + t, :] + s.flat[64 + t : 65 + t, :] for t in range(8)], axis=1)
    block_out[...] = (tokens[...].astype(F32) + bias + total).astype(BF)

    z_sum(zq_sends, s.gq, s.zq, s.tq)
    yq_sends = start(y_sends("yq", s.tq, s.yq))
    wait_recv(small_z)
    s.smallT[...] = s.smallG[pl.ds(zl, 1)][0] + s.smallZ[0] + s.smallZ[1] + s.smallZ[2]
    small_y = start(y_sends("smallY", s.smallT, s.smallY))
    final_forward(g_in)
    final_forward(g_out)
    final_forward(g_dense)

    s.fq[pl.ds(r, 1)] = y_sum(yq_sends, s.tq, s.yq).astype(BF)[None]
    late = start([halves("rq", s.fq)])
    s.smallU[...] = y_sum(small_y, s.smallT, s.smallY)
    small_x = start([make("smallX", d - 1, s.smallU, s.smallX.at[d - 1], along_x(d)) for d in (1, 3, 2)])

    e = owner_total("xE", s.back, s.xE)
    own, inverse = unit_norm(tokens[...].astype(F32))
    mean_e = jnp.mean(e, axis=-1, keepdims=True)
    mean_en = jnp.mean(e * own, axis=-1, keepdims=True)
    tokens_grad[...] = masked_cotangent() + inverse * (e - mean_e - own * mean_en)

    wait_recv(late)
    g_qkv = final_gather("aq", s.fq, o_qkv, by_ctx)
    wait_recv(small_x)
    s.smallV[...] = s.smallU[...] + s.smallX[0] + s.smallX[1] + s.smallX[2]
    small_s = start([make("smallS", 0, s.smallV, s.smallS, sib)])
    final_forward(g_qkv)
    wait_recv(small_s)
    o_small[...] = s.smallV[...] + s.smallS[...]

    for g in (g_in, g_out, g_dense, g_qkv):
        final_finish(g)
    owner_drain("sibO", s.n, s.sibO, "xO", s.xO)
    owner_drain("sibE", s.back, s.sibE, "xE", s.xE)
    for group in (
        finals, small_gather, w1_spread, wo_spread, wd_spread, down_sends, zi_sends, yi_sends, second_sends, second_dense,
        early, zq_sends, yq_sends, late, small_z, small_y, small_x, small_s,
    ):
        wait_send(group)


def block_step(tokens, cot, lens, small_in, m_qkv, m_dense, m_in, m_out):
    vmem = pl.BlockSpec(memory_space=pltpu.VMEM)
    hbm = pl.BlockSpec(memory_space=pl.ANY)
    shapes = [
        jax.ShapeDtypeStruct((R, D), BF), jax.ShapeDtypeStruct((R, D), F32),
        jax.ShapeDtypeStruct((8, 2, 64, QKV), BF), jax.ShapeDtypeStruct((8, 2, 64, UP), BF),
        jax.ShapeDtypeStruct((4, 2, 64, D), BF), jax.ShapeDtypeStruct((2, 64, D), BF),
        jax.ShapeDtypeStruct((16, 128), F32),
    ]
    scratch = [pltpu.VMEM(shape, kind) for shape, kind in VMEM_SHAPES.values()]
    scratch += [pltpu.SemaphoreType.DMA((count,)) for count in SEMS.values()] * 2
    return pl.pallas_call(
        kernel,
        out_shape=shapes,
        in_specs=[vmem, vmem, pl.BlockSpec(memory_space=pltpu.SMEM), vmem, hbm, hbm, hbm, hbm],
        out_specs=[vmem, vmem, hbm, hbm, hbm, hbm, vmem],
        scratch_shapes=scratch,
        compiler_params=pltpu.CompilerParams(
            collective_id=0, has_side_effects=True, vmem_limit_bytes=VMEM_LIMIT),
        name="block_step",
    )(tokens, cot, lens, small_in, m_qkv, m_dense, m_in, m_out)


VMEM_LIMIT = 60 * 2**20


def adam_update(master, first_old, second_old, gradient, rate):
    first_new = BETA_ONE * first_old + (1.0 - BETA_ONE) * gradient
    second_new = BETA_TWO * second_old + (1.0 - BETA_TWO) * gradient * gradient
    first_hat = first_new / (1.0 - BETA_ONE**STEP)
    second_hat = second_new / (1.0 - BETA_TWO**STEP)
    updated = master - rate * (first_hat / (jnp.sqrt(second_hat) + ADAM_EPS) + DECAY * master)
    return gradient, second_new, updated


def per_device(tokens, cotangent, seq_lengths, *state):
    masters, firsts, seconds = state[0:5], state[5:10], state[10:15]
    small_in = jnp.pad(masters[4].reshape(13, 128), ((0, 3), (0, 0)))
    block_out, tokens_grad, g_qkv, g_in, g_out, g_dense, g_small = block_step(
        tokens, cotangent, seq_lengths, small_in, *masters[:4])
    g_qkv = g_qkv.reshape(8, 128, 3, 128).transpose(1, 2, 0, 3).reshape(128, 3 * D)
    g_in = g_in.reshape(4, 2, 128, 4, 128).transpose(2, 3, 1, 0, 4).reshape(128, 4 * D)
    grads = [g_qkv, g_dense.reshape(128, D), g_in, g_out.reshape(512, D), g_small[:13].reshape(-1)]
    results = [
        adam_update(masters[t], firsts[t], seconds[t], grads[t].astype(F32), RATES[t]) for t in range(5)]
    return (block_out, tokens_grad, *(results[t][o] for o in range(3) for t in range(5)))


def solution(mesh):
    seq = P(("rep", "zero", "ctx"), None)
    state = (P("zero", None),) * 4 + (P("zero"),)
    return jax.shard_map(
        per_device,
        mesh=mesh,
        in_specs=(seq, seq, P(("rep", "zero"), None)) + state * 3,
        out_specs=(seq, seq) + state * 3,
        check_vma=False,
    )
```

```python
import functools
import math

import jax
import jax.numpy as jnp
from jax import lax
from jax.experimental import pallas as pl
from jax.experimental.pallas import tpu as pltpu
from jax.sharding import PartitionSpec as P

D = 1024
T = 2048
R = 256
NB = 8
BLOCK = 128
PAIR = 2 * R
EARLY_SECOND = 1
EARLY_WHOLE = 4
STEP = 10
QKV = 384
UP = 512
WIDE = QKV + UP
DOWN = 640
EPSILON = 1e-05
BETA_ONE = 0.9
BETA_TWO = 0.999
ADAM_EPS = 1e-08
DECAY = 0.01
RATES = (0.25, 1.0, 0.25, 0.2, 0.5)
NEG = -1e30
BF = jnp.bfloat16
F32 = jnp.float32
MESH = pl.DeviceIdType.MESH


def nn(a, b):
    return lax.dot_general(a, b, (((1,), (0,)), ((), ())), preferred_element_type=F32)


def nt(a, b):
    return lax.dot_general(a, b, (((1,), (1,)), ((), ())), preferred_element_type=F32)


def rows(block):
    return pl.ds(pl.multiple_of(block * R, R), R)


def span(start, size):
    return pl.ds(pl.multiple_of(start * R, R), size)


def part(index, size):
    return pl.ds(pl.multiple_of(index * size, size), size)


def turns(table):
    lane = lax.broadcasted_iota(jnp.int32, table.shape, 1) % 64
    return jnp.where(lane < 16, table, 1.0), jnp.where(lane < 16, pltpu.roll(table, 112, 1), 0.0)


def rope(u, cosine, sine, sign):
    lane = lax.broadcasted_iota(jnp.int32, u.shape, 1) % 64
    above = pltpu.roll(u, 8, 1)
    below = pltpu.roll(u, u.shape[1] - 8, 1)
    return u * cosine + (sign * jnp.where(lane < 8, -below, above)) * sine


def head_mask(x, head):
    lane = lax.broadcasted_iota(jnp.int32, x.shape, 1)
    return jnp.where((lane >= 64 * head) & (lane < 64 * head + 64), x, jnp.zeros_like(x))


def project(b, s):
    nb = s.n[rows(b), :]
    s.nT[:, rows(b)] = nb.T
    h = nn(nb, s.w1[:, :QKV]) + s.bias[0:1, :QKV]
    cosine, sine = turns(s.turn[rows(b), :])
    s.q[rows(b), :] = (rope(h[:, :128], cosine, sine, 1.0) * 0.125).astype(BF)
    kb = rope(h[:, 128:256], cosine, sine, 1.0).astype(BF)
    vb = h[:, 256:384].astype(BF)
    s.k[rows(b), :] = kb
    s.kT[:, rows(b)] = kb.T
    s.v[rows(b), :] = vb
    s.vT[:, rows(b)] = vb.T
    for t in range(2):
        cols = slice(QKV + 256 * t, QKV + 256 * t + 256)
        hid = slice(128 + 256 * t, 384 + 256 * t)
        x = nn(nb, s.w1[:, cols]) + s.bias[0:1, cols]
        cdf = 0.5 + 0.5 * lax.erf(x * (1 / math.sqrt(2)))
        pdf = jnp.exp(-0.5 * x * x) * (1 / math.sqrt(2 * math.pi))
        act = (x * cdf).astype(BF)
        s.dP[rows(b), cols] = (cdf + x * pdf).astype(BF)
        s.A[rows(b), hid] = act
        s.AT[hid, rows(b)] = act.T


def attend(i, s):
    here = part(i, PAIR)
    qb = s.q[here, :]
    low = s.low[0:1, here]
    heads = [head_mask(qb, h) for h in range(2)]

    def block(j, carry, diagonal=False):
        there = part(j, PAIR)
        key = lax.broadcasted_iota(jnp.int32, (PAIR, PAIR), 0)
        seen = key >= low - j * PAIR
        if diagonal:
            seen = seen & (key <= lax.broadcasted_iota(jnp.int32, (PAIR, PAIR), 1))
        kb = s.k[there, :]
        scores = [jnp.where(seen, nt(kb, heads[h]), NEG) for h in range(2)]
        out = []
        for h in range(2):
            top, total, o = carry[h]
            new = jnp.maximum(top, jnp.max(scores[h], axis=0, keepdims=True))
            p = jnp.exp(scores[h] - new)
            scale = jnp.exp(top - new)
            total = total * scale + jnp.sum(p, axis=0, keepdims=True)
            out.append((new, total, o * scale + nn(s.vT[64 * h : 64 * h + 64, there], p.astype(BF))))
        return tuple(out)

    start = (jnp.full((1, PAIR), NEG, F32), jnp.zeros((1, PAIR), F32), jnp.zeros((64, PAIR), F32))
    carry = lax.fori_loop(0, i, block, block(i, (start, start), True))
    oT = jnp.concatenate([o / total for top, total, o in carry], axis=0).astype(BF)
    s.AT[0:128, here] = oT
    s.A[here, 0:128] = oT.T
    for h in range(2):
        s.lse[h : h + 1, here] = carry[h][0] + jnp.log(carry[h][1])


def pull_down(b, s):
    bb = s.back[rows(b), :]
    d = nt(bb, s.w2[0:128, :]).astype(BF)
    s.dO[rows(b), :] = d
    w = d.astype(F32).T * s.AT[0:128, rows(b)].astype(F32)
    for h in range(2):
        s.lse[2 + h : 3 + h, rows(b)] = jnp.sum(w[64 * h : 64 * h + 64], axis=0, keepdims=True)
    for t in range(2):
        cols = slice(QKV + 256 * t, QKV + 256 * t + 256)
        d = nt(bb, s.w2[128 + 256 * t : 384 + 256 * t, :])
        s.dP[rows(b), cols] = (d * s.dP[rows(b), cols].astype(F32)).astype(BF)


def tile_back(first_query, queries, first_key, keys, s):
    qs, ks = span(first_query, queries), span(first_key, keys)
    qb, db = s.q[qs, :], s.dO[qs, :]
    kb, vb = s.k[ks, :], s.v[ks, :]
    key = lax.broadcasted_iota(jnp.int32, (keys, queries), 0)
    query = lax.broadcasted_iota(jnp.int32, (keys, queries), 1)
    seen = (key >= s.low[0:1, qs] - first_key * R) & (key <= query + (first_query - first_key) * R)
    dk, dv = 0.0, 0.0
    for h in range(2):
        qh, dh = head_mask(qb, h), head_mask(db, h)
        p = jnp.where(seen, jnp.exp(nt(kb, qh) - s.lse[h : h + 1, qs]), 0.0)
        ds = (p * (nt(vb, dh) - s.lse[2 + h : 3 + h, qs])).astype(BF)
        dv = dv + nn(p.astype(BF), dh)
        dk = dk + nn(ds, qh)
        s.dqT[64 * h : 64 * h + 64, qs] += nn(s.kT[64 * h : 64 * h + 64, ks], ds)
    s.dv[ks, :] += dv
    s.dk[ks, :] += dk


def finish_back(b, s):
    cosine, sine = turns(s.turn[rows(b), :])
    s.dP[rows(b), 0:128] = rope(s.dqT[:, rows(b)].T * 0.125, cosine, sine, -1.0).astype(BF)
    s.dP[rows(b), 128:256] = rope(s.dk[rows(b), :], cosine, sine, -1.0).astype(BF)
    s.dP[rows(b), 256:384] = s.dv[rows(b), :].astype(BF)
    s.back[rows(b), :] = nt(s.dP[rows(b), :], s.w1[...]).astype(BF)


def unit_norm(x):
    mean = jnp.mean(x, axis=-1, keepdims=True)
    centered = x - mean
    var = jnp.mean(centered * centered, axis=-1, keepdims=True)
    inv = lax.rsqrt(var + EPSILON)
    return centered * inv, inv


VMEM_SHAPES = dict(
    n=((T, D), BF), nT=((D, T), BF), back=((T, D), BF),
    w1r=((D, WIDE), BF), w1=((D, WIDE), BF), w2=((DOWN, D), BF),
    q=((T, 128), BF), k=((T, 128), BF), v=((T, 128), BF), kT=((128, T), BF), vT=((128, T), BF),
    A=((T, DOWN), BF), AT=((DOWN, T), BF), dP=((T, WIDE), BF), dO=((T, 128), BF),
    dk=((T, 128), F32), dqT=((128, T), F32), dv=((T, 128), F32), lse=((8, T), F32), low=((8, T), jnp.int32),
    angle=((16, T), F32), turn=((T, 128), F32),
    bias=((8, WIDE), F32), flat=((104, 128), F32), cols=((128, 32), F32),
    sibO=((4, R, D), BF), xO=((3, R, D), BF), sibE=((4, R, D), BF), xE=((3, R, D), BF),
    small=((8, 16, 128), F32), flatG=((104, 128), F32), smallG=((2, 4, 16, 128), F32), smallZ=((3, 4, 16, 128), F32),
    smallT=((4, 16, 128), F32), smallY=((3, 16, 128), F32), smallU=((16, 128), F32), smallX=((3, 16, 128), F32),
    smallV=((16, 128), F32), smallS=((16, 128), F32),
    gi=((4, 4, 64, UP), BF), gq=((4, 4, 64, QKV), BF), gd=((2, 64, D), BF), go=((4, 2, 64, D), BF),
    zi=((3, 4, 64, UP), BF), zq=((3, 4, 64, QKV), BF), zd=((3, 64, D), BF), yo=((3, 2, 64, D), BF),
    ti=((4, 64, UP), BF), tq=((4, 64, QKV), BF), td=((64, D), BF), to=((2, 64, D), BF),
    yi=((3, 64, UP), BF), yq=((3, 64, QKV), BF), yd=((3, 64, D), BF), zo=((3, 64, D), BF),
    fi=((4, 2, 64, 128), BF), fq=((3, 2, 64, 128), BF), fd=((2, 64, D), BF), fo=((2, 64, D), BF),
)
SEMS = dict(
    load=23, n=10, back=10, w1=11, wo=11, wd=11, small=7,
    sibO=4, xO=3, sibE=4, xE=3, zi=3, zq=3, zd=3, yo=3, yi=3, yq=3, yd=3, zo=3,
    smallZ=3, smallY=3, smallX=3, smallS=1,
    ri=1, rq=1, rd=1, ro=1, ai=8, aq=8, ao=8, ad=8,
)


class Holder:
    pass


class Transfer:
    def __init__(self, copy, send_if=None, recv_if=None):
        self.copy, self.send_if, self.recv_if = copy, send_if, recv_if

    def only(self, condition, act):
        if condition is None:
            act()
        else:
            pl.when(condition)(act)

    def start(self):
        self.only(self.send_if, self.copy.start)

    def wait_send(self):
        self.only(self.send_if, self.copy.wait_send)

    def wait_recv(self):
        self.only(self.recv_if, self.copy.wait_recv)


def each(f, lo=0, hi=NB):
    def body(i, carry):
        f(i)
        return carry

    lax.fori_loop(lo, hi, body, 0)


def kernel(
    tokens, cot, lens, small_in, m_qkv, m_dense, m_in, m_out,
    block_out, tokens_grad, o_qkv, o_in, o_out, o_dense, o_small, *scratch,
):
    s = Holder()
    it = iter(scratch)
    for name in VMEM_SHAPES:
        setattr(s, name, next(it))
    sends = {name: next(it) for name in SEMS}
    recvs = {name: next(it) for name in SEMS}

    r, z, c = lax.axis_index("rep"), lax.axis_index("zero"), lax.axis_index("ctx")
    y, zl, x, core = z // 2, lax.rem(z, 2), c // 2, lax.rem(c, 2)

    def dev(rr, yy, ll, xx, kk):
        return (rr, yy * 2 + ll, xx * 2 + kk)

    def make(name, index, src, dst, target, send_if=None, recv_if=None):
        copy = pltpu.make_async_remote_copy(
            src_ref=src, dst_ref=dst, send_sem=sends[name].at[index], recv_sem=recvs[name].at[index],
            device_id=target, device_id_type=MESH)
        return Transfer(copy, send_if, recv_if)

    def start(transfers):
        for transfer in transfers:
            transfer.start()
        return transfers

    def wait_recv(transfers):
        for transfer in transfers:
            transfer.wait_recv()

    def wait_send(transfers):
        for transfer in transfers:
            transfer.wait_send()

    def y_at(d):
        return lax.rem(y + d, 4)

    def x_at(d):
        return lax.rem(x + d, 4)

    def z_at(d):
        place = lax.rem(2 * r + zl + d, 4)
        return place // 2, lax.rem(place, 2)

    def along_x(d):
        return dev(r, y, zl, x_at(d), core)

    def along_y(d):
        return dev(r, y_at(d), zl, x, core)

    def along_z(d):
        rr, ll = z_at(d)
        return dev(rr, y, ll, x, core)

    def block_of(xx, kk):
        return xx * 2 + kk

    sib = dev(r, y, zl, x, 1 - core)
    diagonal = z == c
    plane = zl == core
    finals = []

    loads = []

    def load(index, src, dst):
        copy = pltpu.make_async_copy(src, dst, sends["load"].at[index])
        copy.start()
        loads.append(copy)

    for t in range(3):
        load(t, m_qkv.at[:, part(c + 8 * t, 128)], s.dk.at[128 * t : 128 * t + 128, :])
    for t in range(3, 7):
        load(t, m_in.at[:, part((2 * (t - 3) + core) * 4 + x, 128)], s.dk.at[128 * t : 128 * t + 128, :])
    for t in range(8):
        load(7 + t, m_out.at[part(x, 128), 128 * t : 128 * t + 128], s.dv.at[128 * t : 128 * t + 128, :])
        load(15 + t, m_dense.at[:, 128 * t : 128 * t + 128], s.dv.at[D + 128 * t : D + 128 * t + 128, :])

    barrier = pltpu.get_barrier_semaphore()
    peers = [along_x(1), along_x(2), along_x(3), sib]
    for dr in range(2):
        for dy in range(4):
            for dl in range(2):
                if dr or dy or dl:
                    peers.append(dev(lax.rem(r + dr, 2), y_at(dy), lax.rem(zl + dl, 2), x, core))
    for p in peers:
        pl.semaphore_signal(barrier, inc=1, device_id=p, device_id_type=MESH)

    own, inverse = unit_norm(tokens[...].astype(F32))
    s.n[rows(c), :] = own.astype(BF)
    first, second = lens[0, 0], lens[0, 1]
    second_start = (first + BLOCK - 1) // BLOCK * BLOCK

    def masked_cotangent():
        place = lax.broadcasted_iota(jnp.int32, (R, D), 0) + c * R
        valid = (place < first) | ((place >= second_start) & (place < second_start + second))
        return jnp.where(valid, cot[...].astype(F32), 0.0)

    s.back[rows(c), :] = masked_cotangent().astype(BF)
    s.small[pl.ds(z, 1)] = jnp.zeros((1, 16, 128), F32)
    s.small[pl.ds(z, 1), 0:13] = small_in[...].astype(BF).astype(F32)[None]
    for t in range(7):
        loads[t].wait()
        s.w1r[part(z, 128), 128 * t : 128 * t + 128] = s.dk[128 * t : 128 * t + 128, :].astype(BF)
    pl.semaphore_wait(barrier, len(peers))

    lb, rb, ob = block_of(x_at(3), core), block_of(x_at(1), core), block_of(x_at(2), core)

    def gather(name, buf):
        def half(b, h):
            return buf.at[pl.ds(pl.multiple_of(b * R + 128 * h, 128), 128), :]

        def whole(b):
            return buf.at[rows(b), :]

        def same(index, ref, target):
            return make(name, index, ref, ref, target)

        return [
            same(0, half(c, 0), along_x(1)),
            same(1, half(c, 1), along_x(3)),
            same(2, half(c, 1), along_x(1)),
            same(3, half(c, 0), along_x(3)),
            same(4, whole(c), sib),
            same(5, half(lb, 0), along_x(1)),
            same(6, half(rb, 1), along_x(3)),
            same(7, whole(lb), sib),
            same(8, whole(rb), sib),
            same(9, whole(ob), sib),
        ]

    def gather_forward(g):
        for got, sent in ((0, 5), (1, 6), (2, 7), (3, 8)):
            g[got].wait_recv()
            g[sent].start()

    def gather_across(g):
        g[5].wait_recv()
        g[6].wait_recv()
        g[9].start()

    def gather_done(g):
        wait_recv([g[4], g[7], g[8], g[9]])

    n_gather = gather("n", s.n)
    start(n_gather[:5])

    def spread(name, buf, row, same_send=None, same_recv=None, cross_send=None, cross_recv=None):
        out = []
        whole = buf.at[pl.ds(pl.multiple_of(row, 128), 128), :]
        for dy in (1, 3, 2):
            recv_if = same_recv(dy) if same_recv else None
            out.append(make(name, dy - 1, whole, whole, along_y(dy), same_send, recv_if))
        for dy in (0, 1, 3, 2):
            for h in range(2):
                ref = buf.at[pl.ds(pl.multiple_of(row + 64 * h, 64), 64), :]
                target = dev(r if h == 0 else 1 - r, y_at(dy), 1 - zl, x, core)
                recv_if = cross_recv(dy) if cross_recv else None
                out.append(make(name, 3 + 2 * dy + h, ref, ref, target, cross_send, recv_if))
        return out

    small_gather = []
    for dy in range(4):
        for dl in range(2):
            if dy or dl:
                target = dev(r, y_at(dy), lax.rem(zl + dl, 2), x, core)
                small_gather.append(make("small", 2 * dy + dl - 1, s.small.at[z], s.small.at[z], target))
    start(small_gather)
    w1_near, w1_far = [], []
    for dy in range(4):
        row = (y_at(4 - dy) * 2 + zl) * 128
        if dy:
            ref = s.w1r.at[part(z, 128), :]
            w1_near.append(make("w1", dy - 1, ref, ref, along_y(dy)))
        for h in range(2):
            ref = s.w1r.at[pl.ds(pl.multiple_of(row + 64 * h, 64), 64), :]
            target = dev(r if h == 0 else 1 - r, y, 1 - zl, x, core)
            w1_far.append(make("w1", 3 + 2 * dy + h, ref, ref, target))
    start([w1_near[0], w1_near[2], w1_near[1]])
    start(w1_far[0:2])

    lane_place = lax.broadcasted_iota(jnp.int32, (8, T), 1)
    in_first = lane_place < first
    in_second = (lane_place >= second_start) & (lane_place < second_start + second)
    s.low[...] = jnp.where(in_first, 0, jnp.where(in_second, second_start, lane_place))
    position = jnp.where(in_first, lane_place, jnp.where(in_second, lane_place - second_start, 0))
    entry = lax.broadcasted_iota(jnp.int32, (8, T), 0)
    frequency = jnp.zeros((8, T), F32)
    for t in range(8):
        frequency = jnp.where(entry == t, 10000.0 ** (-t / 8), frequency)
    turn = position.astype(F32) * frequency
    s.angle[0:8, :] = jnp.cos(turn)
    s.angle[8:16, :] = jnp.sin(turn)

    def tables(b):
        cs, sn = s.angle[0:8, rows(b)], s.angle[8:16, rows(b)]
        rest = jnp.zeros((32, R), F32)
        s.turn[rows(b), :] = jnp.concatenate([cs, cs, sn, sn, rest] * 2, axis=0).T

    each(tables)
    s.flatG[...] = jnp.zeros_like(s.flatG)
    s.smallG[...] = jnp.zeros_like(s.smallG)

    for dy in (1, 3, 2):
        w1_near[dy - 1].wait_recv()
        start(w1_far[2 * dy : 2 * dy + 2])
    gather_forward(n_gather)
    back_gather = gather("back", s.back)
    start(back_gather[:5])

    for t in range(7, 23):
        loads[t].wait()
    wo_row = 128 + y * 128
    wo_spread = spread("wo", s.w2, wo_row, plane, lambda dy: plane, plane, lambda dy: zl != core)

    def dense_from(dy):
        return lax.rem(y + 4 - dy, 4) == x

    wd_spread = spread(
        "wd", s.w2, 0, diagonal, lambda dy: dense_from(dy) & plane, diagonal, lambda dy: dense_from(dy) & (zl != core))

    @pl.when(plane)
    def _():
        for t in range(8):
            cols = slice(128 * t, 128 * t + 128)
            s.w2[pl.ds(pl.multiple_of(wo_row, 128), 128), cols] = s.dv[128 * t : 128 * t + 128, :].astype(BF)

    @pl.when(diagonal)
    def _():
        for t in range(8):
            s.w2[0:128, 128 * t : 128 * t + 128] = s.dv[D + 128 * t : D + 128 * t + 128, :].astype(BF)

    s.dk[...] = jnp.zeros_like(s.dk)
    s.dv[...] = jnp.zeros_like(s.dv)
    s.dqT[...] = jnp.zeros_like(s.dqT)
    start(wd_spread)
    start(wo_spread)

    wait_recv(small_gather)
    for t in range(8):
        s.flat[13 * t : 13 * t + 13, :] = s.small[t, 0:13, :]
    s.cols[...] = s.flat[0:32, :].T
    wait_recv(w1_far)

    def line(at):
        return jnp.concatenate([s.flat[at + t : at + t + 1, :] for t in range(8)], axis=1)

    shifts = jnp.concatenate([line(8), line(24), jnp.zeros((6, D), F32)], axis=0).astype(BF)
    turned = nn(shifts, s.w1r[...])
    for t in range(3):
        cols = slice(128 * t, 128 * t + 128)
        s.bias[0:1, cols] = turned[0:1, cols] + s.flat[pl.ds(32 + 8 * t + c, 1), :]
    for t in range(4):
        cols = slice(QKV + 128 * t, QKV + 128 * t + 128)
        s.bias[0:1, cols] = turned[1:2, cols] + s.flat[pl.ds(72 + (2 * t + core) * 4 + x, 1), :]
    for t in range(8):
        sl = slice(128 * t, 128 * t + 128)
        s.w1[sl, :QKV] = (s.w1r[sl, :QKV].astype(F32) * s.cols[:, t : t + 1]).astype(BF)
        s.w1[sl, QKV:] = (s.w1r[sl, QKV:].astype(F32) * s.cols[:, 16 + t : 17 + t]).astype(BF)

    wait_recv(n_gather[4:5])

    def project_turn(t):
        p, q = t // 2, lax.rem(t, 2)

        @pl.when(t == 4)
        def _():
            gather_across(n_gather)
            wait_recv(n_gather[7:9])

        @pl.when(t == 6)
        def _():
            wait_recv(n_gather[9:])

        middle = lax.rem((p + 1) // 2, 2)
        dx = middle * (3 - 2 * q) + (1 - middle) * 2 * (p // 3)
        dk = middle * (p - 1) + (1 - middle) * q
        project(block_of(x_at(dx), lax.rem(core + dk, 2)), s)

    each(project_turn)
    gather_forward(back_gather)

    def to_sibling(name, buf, slots, xx):
        return make(name, xx, buf.at[rows(block_of(xx, 1 - core)), :], slots.at[xx], sib)

    def to_owner(name, buf, slots, xx, d):
        return make(name, d - 1, buf.at[rows(block_of(xx, core)), :], slots.at[d - 1], dev(r, y, zl, xx, core))

    def owner_sum(name, buf, slots, name_x, slots_x, xx):
        to_sibling(name, buf, slots, xx).wait_recv()
        mine = buf[rows(block_of(xx, core)), :].astype(F32) + slots[pl.ds(xx, 1)][0].astype(F32)
        buf[rows(block_of(xx, core)), :] = mine.astype(BF)

        @pl.when(xx != x)
        def _():
            to_owner(name_x, buf, slots_x, xx, lax.rem(x + 4 - xx, 4)).start()

    def owner_total(name_x, buf, slots_x):
        total = buf[rows(c), :].astype(F32)
        for d in (1, 3, 2):
            to_owner(name_x, buf, slots_x, x_at(4 - d), d).wait_recv()
            total = total + slots_x[d - 1].astype(F32)
        return total

    def owner_drain(name, buf, slots, name_x, slots_x):
        for xx in range(4):
            to_sibling(name, buf, slots, xx).wait_send()
        for d in (1, 2, 3):
            to_owner(name_x, buf, slots_x, x_at(4 - d), d).wait_send()

    def down(i):
        s.n[rows(i), :] = nn(s.A[rows(i), :], s.w2[...]).astype(BF)

    def down_first(xx):
        down(block_of(xx, 1 - core))
        to_sibling("sibO", s.n, s.sibO, xx).start()


    def attend_turn(i):
        @pl.when(i == 3)
        def _():
            gather_across(back_gather)

        attend(i, s)

    each(attend_turn, 0, 4)
    wait_send(n_gather)
    wait_recv(wd_spread)
    wait_recv(wo_spread)
    each(down_first, 0, 4)
    each(lambda xx: down(block_of(xx, core)), 0, 4)
    gather_done(back_gather)
    each(lambda b: pull_down(b, s), 0, 4)
    each(lambda xx: owner_sum("sibO", s.n, s.sibO, "xO", s.xO, xx), 0, 4)
    each(lambda b: pull_down(b, s), 4, 8)

    def grad_down(t):
        cols = part(t, 256)
        g = nn(s.AT[...], s.back[:, cols]).astype(BF)
        for h in range(2):
            s.gd[h, :, cols] = g[64 * h : 64 * h + 64]
            for yy in range(4):
                s.go[yy, h, :, cols] = g[128 + 128 * yy + 64 * h : 192 + 128 * yy + 64 * h]

    each(grad_down, 0, 4)

    def down_grads_out():
        out = [make("yo", d - 1, s.go.at[y_at(d)], s.yo.at[d - 1], along_y(d)) for d in (1, 3, 2)]
        for d in (1, 3, 2):
            rr, ll = z_at(d)
            out.append(make("zd", d - 1, s.gd.at[rr], s.zd.at[d - 1], along_z(d), ll == core, plane))
        return out

    down_sends = start(down_grads_out())

    def grad_up(lo, hi, out, at, gain_at, shift_at):
        g = nn(s.nT[...], s.dP[:, lo:hi])
        total = jnp.sum(s.dP[:, lo:hi].astype(F32), axis=0, keepdims=True)
        gains, moves = [], []
        for t in range(8):
            sl = slice(128 * t, 128 * t + 128)
            w = s.w1r[sl, lo:hi].astype(F32)
            gains.append(jnp.sum(w * g[sl], axis=1, keepdims=True))
            moves.append(jnp.sum(w * total, axis=1, keepdims=True))
            full = g[sl] * s.cols[:, gain_at + t : gain_at + t + 1] + s.cols[:, shift_at + t : shift_at + t + 1] * total
            for h in range(2):
                out[2 * h + t % 2, t // 2, :, at : at + hi - lo] = full[64 * h : 64 * h + 64].astype(BF)
        return total, jnp.concatenate(gains, axis=1), jnp.concatenate(moves, axis=1)

    total_a, gain_a, move_a = grad_up(QKV, QKV + 256, s.gi, 0, 16, 24)
    total_b, gain_b, move_b = grad_up(QKV + 256, WIDE, s.gi, 256, 16, 24)
    s.flatG[16:32, :] = jnp.concatenate([gain_a + gain_b, move_a + move_b], axis=1).T
    for t in range(4):
        total = total_a if t < 2 else total_b
        at = 128 * (t % 2)
        s.flatG[pl.ds(72 + (2 * t + core) * 4 + x, 1), :] = total[:, at : at + 128]
    back_sum = jnp.sum(s.back[rows(c), :].astype(F32), axis=0, keepdims=True)
    for t in range(8):
        s.flatG[56 + t : 57 + t, :] = back_sum[:, 128 * t : 128 * t + 128]
        s.flatG[64 + t : 65 + t, :] = back_sum[:, 128 * t : 128 * t + 128]

    def z_sends(name, src, slots):
        return [make(name, d - 1, src.at[2 * z_at(d)[0] + z_at(d)[1]], slots.at[d - 1], along_z(d)) for d in (1, 3, 2)]

    def y_sends(name, src, slots):
        return [make(name, d - 1, src.at[y_at(d)], slots.at[d - 1], along_y(d)) for d in (1, 3, 2)]

    def z_sum(transfers, src, slots, out):
        wait_recv(transfers)
        mine = src[pl.ds(2 * r + zl, 1)][0].astype(F32)
        for d in range(3):
            mine = mine + slots[d].astype(F32)
        out[...] = mine.astype(out.dtype)

    def y_sum(transfers, src, slots):
        wait_recv(transfers)
        mine = src[pl.ds(y, 1)][0].astype(F32)
        for d in range(3):
            mine = mine + slots[d].astype(F32)
        return mine

    zi_sends = start(z_sends("zi", s.gi, s.zi))
    wait_send(back_gather)

    def turn_x(t):
        return 3 - lax.rem(t, 4)

    def turn_core(t):
        return lax.rem(turn_x(t) + t // 4, 2)

    def back_sum(t):
        @pl.when(turn_core(t) == core)
        def _():
            owner_sum("sibE", s.back, s.sibE, "xE", s.xE, turn_x(t))

    def back_step(t):
        b = block_of(turn_x(t), turn_core(t))
        late = t // 4
        row_pairs = (4 - t) * (1 - late) + (4 - t // 2) * late
        column_pairs = ((t + 1) // 2) * (1 - late)
        each(lambda l: tile_back(b, R, late + (2 + 2 * late) * l, PAIR, s), 0, row_pairs)
        each(lambda l: tile_back(5 - 4 * (column_pairs - 1) + 4 * l, PAIR, b, R, s), 0, column_pairs)
        finish_back(b, s)

        @pl.when(turn_core(t) != core)
        def _():
            to_sibling("sibE", s.back, s.sibE, turn_x(t)).start()

        @pl.when(t > 0)
        def _():
            back_sum(t - 1)

    def final_gather(name, buf, out, slot, source=None):
        def has(xx, kk):
            return source(xx, kk) if source else None

        def at(xx, kk):
            return slot(out, xx, kk)

        local = pltpu.make_async_copy(buf, at(x, core), sends[name].at[7])
        first_hop = [
            make(name, d - 1, buf, at(x, core), along_x(d), has(x, core), has(x_at(4 - d), core)) for d in (1, 3, 2)]
        first_hop.append(make(name, 3, buf, at(x, core), sib, has(x, core), has(x, 1 - core)))
        second_hop = []
        for d in (1, 3, 2):
            xx = x_at(4 - d)
            ref = at(xx, core)
            second_hop.append(make(name, 3 + d, ref, ref, sib, has(xx, core), has(xx, 1 - core)))
        own_copy = Transfer(local, has(x, core))
        own_copy.start()
        start(first_hop)
        return own_copy, first_hop, second_hop

    def final_forward(g):
        own_copy, first_hop, second_hop = g
        for got, sent in zip(first_hop[:3], second_hop):
            got.wait_recv()
            sent.start()

    def final_finish(g):
        own_copy, first_hop, second_hop = g
        own_copy.only(own_copy.send_if, own_copy.copy.wait)
        first_hop[3].wait_recv()
        wait_recv(second_hop)
        finals.extend(first_hop + second_hop)

    yi_sends = y_sends("yi", s.ti, s.yi)
    second_sends = []
    for d in (1, 3, 2):
        rr, ll = z_at(d)
        second_sends.append(make("zo", d - 1, s.to.at[rr], s.zo.at[d - 1], along_z(d), ll == core, plane))

    def to_diagonal(d):
        return make("yd", d - 1, s.td, s.yd.at[d - 1], along_y(d), plane & (y_at(d) == x), diagonal)

    second_dense = [to_diagonal(d) for d in (1, 3, 2)]

    def early_second():
        z_sum(zi_sends, s.gi, s.zi, s.ti)
        start(yi_sends)
        wait_recv(down_sends)
        total = s.go[pl.ds(y, 1)][0].astype(F32) + s.yo[0].astype(F32) + s.yo[1].astype(F32) + s.yo[2].astype(F32)
        s.to[...] = total.astype(BF)

        @pl.when(plane)
        def _():
            mine = s.gd[pl.ds(r, 1)][0].astype(F32)
            for d in range(3):
                mine = mine + s.zd[d].astype(F32)
            s.td[...] = mine.astype(BF)

        start(second_sends)
        start(second_dense)

    other = dev(1 - r, y, zl, x, core)

    def halves(name, buf, condition=None):
        ref = buf.at[r] if len(buf.shape) == 3 else buf.at[:, r]
        return make(name, 0, ref, ref, other, condition, condition)

    def in_blocks(value, buf):
        for t in range(buf.shape[0]):
            buf[t, pl.ds(r, 1)] = value[:, 128 * t : 128 * t + 128].astype(BF)[None]

    early = [halves("ri", s.fi), halves("ro", s.fo, plane), halves("rd", s.fd, diagonal)]

    def early_whole():
        in_blocks(y_sum(yi_sends, s.ti, s.yi), s.fi)
        wait_recv(second_sends)
        wait_recv(second_dense)

        @pl.when(plane)
        def _():
            mine = s.to[pl.ds(r, 1)][0].astype(F32)
            for d in range(3):
                mine = mine + s.zo[d].astype(F32)
            s.fo[pl.ds(r, 1)] = mine.astype(BF)[None]

        @pl.when(diagonal)
        def _():
            mine = s.td[...].astype(F32)
            for d in range(3):
                mine = mine + s.yd[d].astype(F32)
            s.fd[pl.ds(r, 1)] = mine.astype(BF)[None]
        start(early)

    def back_turn(t):
        back_step(t)
        pl.when(t == EARLY_SECOND)(early_second)
        pl.when(t == EARLY_WHOLE)(early_whole)

    each(back_turn)
    back_sum(7)
    wait_recv(early)
    g_in = final_gather("ai", s.fi, o_in, lambda out, xx, kk: out.at[:, kk, xx])
    g_out = final_gather("ao", s.fo, o_out, lambda out, xx, kk: out.at[xx], lambda xx, kk: zl == kk)
    g_dense = final_gather("ad", s.fd, o_dense, lambda out, xx, kk: out, lambda xx, kk: (zl == kk) & (y == xx))


    total_q, gain_q, move_q = grad_up(0, 256, s.gq, 0, 0, 8)
    total_v, gain_v, move_v = grad_up(256, QKV, s.gq, 256, 0, 8)
    zq_sends = start(z_sends("zq", s.gq, s.zq))
    s.flatG[0:16, :] = jnp.concatenate([gain_q + gain_v, move_q + move_v], axis=1).T
    s.flatG[pl.ds(32 + c, 1), :] = total_q[:, 0:128]
    s.flatG[pl.ds(40 + c, 1), :] = total_q[:, 128:256]
    s.flatG[pl.ds(48 + c, 1), :] = total_v
    for t in range(8):
        s.smallG[t % 2, t // 2, 0:13, :] = s.flatG[13 * t : 13 * t + 13, :]
    small_z = start([make("smallZ", d - 1, s.smallG.at[z_at(d)[1]], s.smallZ.at[d - 1], along_z(d)) for d in (1, 3, 2)])

    total = owner_total("xO", s.n, s.xO)
    bias = jnp.concatenate([s.flat[56 + t : 57 + t, :] + s.flat[64 + t : 65 + t, :] for t in range(8)], axis=1)
    block_out[...] = (tokens[...].astype(F32) + bias + total).astype(BF)

    z_sum(zq_sends, s.gq, s.zq, s.tq)
    yq_sends = start(y_sends("yq", s.tq, s.yq))
    wait_recv(small_z)
    s.smallT[...] = s.smallG[pl.ds(zl, 1)][0] + s.smallZ[0] + s.smallZ[1] + s.smallZ[2]
    small_y = start(y_sends("smallY", s.smallT, s.smallY))
    in_blocks(y_sum(yq_sends, s.tq, s.yq), s.fq)
    late = start([halves("rq", s.fq)])
    s.smallU[...] = y_sum(small_y, s.smallT, s.smallY)
    small_x = start([make("smallX", d - 1, s.smallU, s.smallX.at[d - 1], along_x(d)) for d in (1, 3, 2)])

    wait_recv(late)
    g_qkv = final_gather("aq", s.fq, o_qkv, lambda out, xx, kk: out.at[:, block_of(xx, kk)])
    final_forward(g_in)
    final_forward(g_out)
    final_forward(g_dense)

    e = owner_total("xE", s.back, s.xE)
    own, inverse = unit_norm(tokens[...].astype(F32))
    mean_e = jnp.mean(e, axis=-1, keepdims=True)
    mean_en = jnp.mean(e * own, axis=-1, keepdims=True)
    tokens_grad[...] = masked_cotangent() + inverse * (e - mean_e - own * mean_en)

    wait_recv(small_x)
    s.smallV[...] = s.smallU[...] + s.smallX[0] + s.smallX[1] + s.smallX[2]
    small_s = start([make("smallS", 0, s.smallV, s.smallS, sib)])
    final_forward(g_qkv)
    wait_recv(small_s)
    o_small[...] = s.smallV[...] + s.smallS[...]

    for g in (g_in, g_out, g_dense, g_qkv):
        final_finish(g)
    owner_drain("sibO", s.n, s.sibO, "xO", s.xO)
    owner_drain("sibE", s.back, s.sibE, "xE", s.xE)
    for group in (
        finals, small_gather, w1_near, w1_far, wo_spread, wd_spread, down_sends, zi_sends, yi_sends, second_sends, second_dense,
        early, zq_sends, yq_sends, late, small_z, small_y, small_x, small_s,
    ):
        wait_send(group)


def block_step(tokens, cot, lens, small_in, m_qkv, m_dense, m_in, m_out):
    vmem = pl.BlockSpec(memory_space=pltpu.VMEM)
    hbm = pl.BlockSpec(memory_space=pl.ANY)
    shapes = [
        jax.ShapeDtypeStruct((R, D), BF), jax.ShapeDtypeStruct((R, D), F32),
        jax.ShapeDtypeStruct((3, 8, 2, 64, 128), BF), jax.ShapeDtypeStruct((4, 2, 4, 2, 64, 128), BF),
        jax.ShapeDtypeStruct((4, 2, 64, D), BF), jax.ShapeDtypeStruct((2, 64, D), BF),
        jax.ShapeDtypeStruct((16, 128), F32),
    ]
    scratch = [pltpu.VMEM(shape, kind) for shape, kind in VMEM_SHAPES.values()]
    scratch += [pltpu.SemaphoreType.DMA((count,)) for count in SEMS.values()] * 2
    return pl.pallas_call(
        kernel,
        out_shape=shapes,
        in_specs=[vmem, vmem, pl.BlockSpec(memory_space=pltpu.SMEM), vmem, hbm, hbm, hbm, hbm],
        out_specs=[vmem, vmem, hbm, hbm, hbm, hbm, vmem],
        scratch_shapes=scratch,
        compiler_params=pltpu.CompilerParams(
            collective_id=0, has_side_effects=True, vmem_limit_bytes=VMEM_LIMIT),
        name="block_step",
    )(tokens, cot, lens, small_in, m_qkv, m_dense, m_in, m_out)


VMEM_LIMIT = 60 * 2**20


def adam_update(master, first_old, second_old, gradient, rate):
    first_new = BETA_ONE * first_old + (1.0 - BETA_ONE) * gradient
    second_new = BETA_TWO * second_old + (1.0 - BETA_TWO) * gradient * gradient
    first_hat = first_new / (1.0 - BETA_ONE**STEP)
    second_hat = second_new / (1.0 - BETA_TWO**STEP)
    updated = master - rate * (first_hat / (jnp.sqrt(second_hat) + ADAM_EPS) + DECAY * master)
    return gradient, second_new, updated


def adam_chunks():
    cols = [(0, b, 6) for b in range(0, 24, 6)] + [(2, b, 8) for b in range(0, 32, 8)]
    out = [(t, (slice(None), slice(128 * b, 128 * (b + n))), slice(b, b + n)) for t, b, n in cols]
    out += [(3, slice(128 * b, 128 * b + 128), slice(128 * b, 128 * b + 128)) for b in range(4)]
    return out + [(1, slice(None), slice(None)), (4, slice(None), slice(0, 13))]


def adam_kernel(*refs):
    grads, state, outs = refs[:5], refs[5:20], refs[20:35]
    grad_vmem, state_vmem = refs[35:40], refs[40:55]
    in_sem, out_sem = refs[55], refs[56]
    chunks = adam_chunks()
    loads, stores = [], []
    for n, (t, at, grad_at) in enumerate(chunks):
        group = [pltpu.make_async_copy(grads[t].at[grad_at], grad_vmem[t].at[grad_at], in_sem.at[n, 3])]
        for o in range(3):
            k = 5 * o + t
            group.append(pltpu.make_async_copy(state[k].at[at], state_vmem[k].at[at], in_sem.at[n, o]))
        for copy in group:
            copy.start()
        loads.append(group)
    for n, (t, at, grad_at) in enumerate(chunks):
        for copy in loads[n]:
            copy.wait()
        bufs = [state_vmem[5 * o + t] for o in range(3)]

        def step(where, gradient, t=t, bufs=bufs):
            master, first, second = (buf[where] for buf in bufs)
            _, renewed, updated = adam_update(master, first, second, gradient, RATES[t])
            bufs[0][where], bufs[1][where], bufs[2][where] = updated, gradient, renewed

        if t in (0, 2):
            for b in range(grad_at.start, grad_at.stop):
                step((slice(None), slice(128 * b, 128 * b + 128)), grad_vmem[t][b].astype(F32))
        else:
            step((at, slice(None)), grad_vmem[t][grad_at, :].astype(F32))
        for o, buf in ((0, bufs[1]), (1, bufs[2]), (2, bufs[0])):
            copy = pltpu.make_async_copy(buf.at[at], outs[5 * o + t].at[at], out_sem.at[n, o])
            copy.start()
            stores.append(copy)
    for copy in stores:
        copy.wait()


def adam_step(grads, state):
    hbm = pl.BlockSpec(memory_space=pl.ANY)
    count = len(adam_chunks())
    return pl.pallas_call(
        adam_kernel,
        out_shape=[jax.ShapeDtypeStruct(a.shape, F32) for a in state],
        in_specs=[hbm] * 20,
        out_specs=[hbm] * 15,
        scratch_shapes=[pltpu.VMEM(a.shape, a.dtype) for a in (*grads, *state)]
        + [pltpu.SemaphoreType.DMA((count, 4)), pltpu.SemaphoreType.DMA((count, 3))],
        compiler_params=pltpu.CompilerParams(vmem_limit_bytes=VMEM_LIMIT),
        name="adam_step",
    )(*grads, *state)


def per_device(tokens, cotangent, seq_lengths, *state):
    state = [a.reshape(13, 128) if a.ndim == 1 else a for a in state]
    block_out, tokens_grad, g_qkv, g_in, g_out, g_dense, g_small = block_step(
        tokens, cotangent, seq_lengths, state[4], *state[:4])
    grads = [
        g_qkv.reshape(24, 128, 128), g_dense.reshape(128, D), g_in.reshape(32, 128, 128), g_out.reshape(512, D), g_small]
    results = [a.reshape(-1) if a.shape[0] == 13 else a for a in adam_step(grads, state)]
    return (block_out, tokens_grad, *results)


def solution(mesh):
    seq = P(("rep", "zero", "ctx"), None)
    state = (P("zero", None),) * 4 + (P("zero"),)
    return jax.shard_map(
        per_device,
        mesh=mesh,
        in_specs=(seq, seq, P(("rep", "zero"), None)) + state * 3,
        out_specs=(seq, seq) + state * 3,
        check_vma=False,
    )
```

```python
import functools
import math

import jax
import jax.numpy as jnp
from jax import lax
from jax.experimental import pallas as pl
from jax.experimental.pallas import tpu as pltpu
from jax.sharding import PartitionSpec as P

D = 1024
T = 2048
R = 256
NB = 8
BLOCK = 128
PAIR = 2 * R
EARLY_SECOND = 3
EARLY_WHOLE = 6
EARLY_GATHER = 7
STEP = 10
QKV = 384
UP = 512
WIDE = QKV + UP
DOWN = 640
EPSILON = 1e-05
BETA_ONE = 0.9
BETA_TWO = 0.999
ADAM_EPS = 1e-08
DECAY = 0.01
RATES = (0.25, 1.0, 0.25, 0.2, 0.5)
NEG = -1e30
BF = jnp.bfloat16
F32 = jnp.float32
MESH = pl.DeviceIdType.MESH


def nn(a, b):
    return lax.dot_general(a, b, (((1,), (0,)), ((), ())), preferred_element_type=F32)


def nt(a, b):
    return lax.dot_general(a, b, (((1,), (1,)), ((), ())), preferred_element_type=F32)


def rows(block):
    return pl.ds(pl.multiple_of(block * R, R), R)


def span(start, size):
    return pl.ds(pl.multiple_of(start * R, R), size)


def part(index, size):
    return pl.ds(pl.multiple_of(index * size, size), size)


def turns(table):
    lane = lax.broadcasted_iota(jnp.int32, table.shape, 1) % 64
    return jnp.where(lane < 16, table, 1.0), jnp.where(lane < 16, pltpu.roll(table, 112, 1), 0.0)


def rope(u, cosine, sine, sign):
    lane = lax.broadcasted_iota(jnp.int32, u.shape, 1) % 64
    above = pltpu.roll(u, 8, 1)
    below = pltpu.roll(u, u.shape[1] - 8, 1)
    return u * cosine + (sign * jnp.where(lane < 8, -below, above)) * sine


def head_mask(x, head):
    lane = lax.broadcasted_iota(jnp.int32, x.shape, 1)
    return jnp.where((lane >= 64 * head) & (lane < 64 * head + 64), x, jnp.zeros_like(x))


def project(b, s):
    nb = s.n[rows(b), :]
    s.nT[:, rows(b)] = nb.T
    h = nn(nb, s.w1[:, :QKV]) + s.bias[0:1, :QKV]
    cosine, sine = turns(s.turn[rows(b), :])
    s.q[rows(b), :] = (rope(h[:, :128], cosine, sine, 1.0) * 0.125).astype(BF)
    kb = rope(h[:, 128:256], cosine, sine, 1.0).astype(BF)
    vb = h[:, 256:384].astype(BF)
    s.k[rows(b), :] = kb
    s.kT[:, rows(b)] = kb.T
    s.v[rows(b), :] = vb
    s.vT[:, rows(b)] = vb.T
    for t in range(2):
        cols = slice(QKV + 256 * t, QKV + 256 * t + 256)
        hid = slice(128 + 256 * t, 384 + 256 * t)
        x = nn(nb, s.w1[:, cols]) + s.bias[0:1, cols]
        cdf = 0.5 + 0.5 * lax.erf(x * (1 / math.sqrt(2)))
        pdf = jnp.exp(-0.5 * x * x) * (1 / math.sqrt(2 * math.pi))
        act = (x * cdf).astype(BF)
        s.dP[rows(b), cols] = (cdf + x * pdf).astype(BF)
        s.A[rows(b), hid] = act
        s.AT[hid, rows(b)] = act.T


def attend(i, s):
    here = part(i, PAIR)
    qb = s.q[here, :]
    low = s.low[0:1, here]
    heads = [head_mask(qb, h) for h in range(2)]

    def block(j, carry, diagonal=False):
        there = part(j, PAIR)
        key = lax.broadcasted_iota(jnp.int32, (PAIR, PAIR), 0)
        seen = key >= low - j * PAIR
        if diagonal:
            seen = seen & (key <= lax.broadcasted_iota(jnp.int32, (PAIR, PAIR), 1))
        kb = s.k[there, :]
        scores = [jnp.where(seen, nt(kb, heads[h]), NEG) for h in range(2)]
        out = []
        for h in range(2):
            top, total, o = carry[h]
            new = jnp.maximum(top, jnp.max(scores[h], axis=0, keepdims=True))
            p = jnp.exp(scores[h] - new)
            scale = jnp.exp(top - new)
            total = total * scale + jnp.sum(p, axis=0, keepdims=True)
            out.append((new, total, o * scale + nn(s.vT[64 * h : 64 * h + 64, there], p.astype(BF))))
        return tuple(out)

    start = (jnp.full((1, PAIR), NEG, F32), jnp.zeros((1, PAIR), F32), jnp.zeros((64, PAIR), F32))
    carry = lax.fori_loop(0, i, block, block(i, (start, start), True))
    oT = jnp.concatenate([o / total for top, total, o in carry], axis=0).astype(BF)
    s.AT[0:128, here] = oT
    s.A[here, 0:128] = oT.T
    for h in range(2):
        s.lse[h : h + 1, here] = carry[h][0] + jnp.log(carry[h][1])


def pull_down(b, s):
    bb = s.back[rows(b), :]
    d = nt(bb, s.w2[0:128, :]).astype(BF)
    s.dO[rows(b), :] = d
    w = d.astype(F32).T * s.AT[0:128, rows(b)].astype(F32)
    for h in range(2):
        s.lse[2 + h : 3 + h, rows(b)] = jnp.sum(w[64 * h : 64 * h + 64], axis=0, keepdims=True)
    for t in range(2):
        cols = slice(QKV + 256 * t, QKV + 256 * t + 256)
        d = nt(bb, s.w2[128 + 256 * t : 384 + 256 * t, :])
        s.dP[rows(b), cols] = (d * s.dP[rows(b), cols].astype(F32)).astype(BF)


def tile_back(first_query, queries, first_key, keys, s):
    qs, ks = span(first_query, queries), span(first_key, keys)
    qb, db = s.q[qs, :], s.dO[qs, :]
    kb, vb = s.k[ks, :], s.v[ks, :]
    key = lax.broadcasted_iota(jnp.int32, (keys, queries), 0)
    query = lax.broadcasted_iota(jnp.int32, (keys, queries), 1)
    seen = (key >= s.low[0:1, qs] - first_key * R) & (key <= query + (first_query - first_key) * R)
    dk, dv = 0.0, 0.0
    for h in range(2):
        qh, dh = head_mask(qb, h), head_mask(db, h)
        p = jnp.where(seen, jnp.exp(nt(kb, qh) - s.lse[h : h + 1, qs]), 0.0)
        ds = (p * (nt(vb, dh) - s.lse[2 + h : 3 + h, qs])).astype(BF)
        dv = dv + nn(p.astype(BF), dh)
        dk = dk + nn(ds, qh)
        s.dqT[64 * h : 64 * h + 64, qs] += nn(s.kT[64 * h : 64 * h + 64, ks], ds)
    s.dv[ks, :] += dv
    s.dk[ks, :] += dk


def finish_back(b, s):
    cosine, sine = turns(s.turn[rows(b), :])
    s.dP[rows(b), 0:128] = rope(s.dqT[:, rows(b)].T * 0.125, cosine, sine, -1.0).astype(BF)
    s.dP[rows(b), 128:256] = rope(s.dk[rows(b), :], cosine, sine, -1.0).astype(BF)
    s.dP[rows(b), 256:384] = s.dv[rows(b), :].astype(BF)
    s.back[rows(b), :] = nt(s.dP[rows(b), :], s.w1[...]).astype(BF)


def unit_norm(x):
    mean = jnp.mean(x, axis=-1, keepdims=True)
    centered = x - mean
    var = jnp.mean(centered * centered, axis=-1, keepdims=True)
    inv = lax.rsqrt(var + EPSILON)
    return centered * inv, inv


VMEM_SHAPES = dict(
    n=((T, D), BF), nT=((D, T), BF), back=((T, D), BF),
    w1r=((D, WIDE), BF), w1=((D, WIDE), BF), w2=((DOWN, D), BF),
    q=((T, 128), BF), k=((T, 128), BF), v=((T, 128), BF), kT=((128, T), BF), vT=((128, T), BF),
    A=((T, DOWN), BF), AT=((DOWN, T), BF), dP=((T, WIDE), BF), dO=((T, 128), BF),
    dk=((T, 128), F32), dqT=((128, T), F32), dv=((T, 128), F32), lse=((8, T), F32), low=((8, T), jnp.int32),
    angle=((16, T), F32), turn=((T, 128), F32),
    bias=((8, WIDE), F32), flat=((104, 128), F32), cols=((128, 32), F32),
    sibO=((4, R, D), BF), nearO=((3, R, D), BF), sibE=((4, R, D), BF), nearE=((3, R, D), BF),
    small=((8, 16, 128), F32), flatG=((104, 128), F32), smallG=((2, 4, 16, 128), F32), smallZ=((3, 4, 16, 128), F32),
    smallT=((4, 16, 128), F32), smallY=((3, 16, 128), F32), smallU=((16, 128), F32), smallX=((3, 16, 128), F32),
    smallV=((16, 128), F32), smallS=((16, 128), F32),
    gi=((4, 4, 64, UP), BF), gq=((4, 4, 64, 256), BF), gv=((4, 4, 64, 128), BF), gd=((2, 64, D), BF), go=((4, 2, 64, D), BF),
    zi=((3, 4, 64, UP), BF), zq=((3, 4, 64, 256), BF), yv=((3, 4, 64, 128), BF), zd=((3, 64, D), BF), yo=((3, 2, 64, D), BF),
    ti=((4, 64, UP), BF), tq=((4, 64, 256), BF), tv=((4, 64, 128), BF), td=((64, D), BF), to=((2, 64, D), BF),
    yi=((3, 64, UP), BF), yq=((3, 64, 256), BF), zv=((3, 64, 128), BF), yd=((3, 64, D), BF), zo=((3, 64, D), BF),
    fi=((4, 2, 64, 128), BF), fq=((3, 2, 64, 128), BF), fd=((2, 64, D), BF), fo=((2, 64, D), BF),
)
SEMS = dict(
    load=23, n=10, back=10, w1=11, wo=11, wd=11, small=7,
    sibO=4, nearO=3, sibE=4, nearE=3, zi=3, zq=3, yv=3, zv=3, zd=3, yo=3, yi=3, yq=3, yd=3, zo=3,
    smallZ=3, smallY=3, smallX=3, smallS=1,
    ri=1, rq=1, rd=1, ro=1, ai=8, aq=8, ao=8, ad=8,
)


class Holder:
    pass


class Transfer:
    def __init__(self, copy, send_if=None, recv_if=None):
        self.copy, self.send_if, self.recv_if = copy, send_if, recv_if

    def only(self, condition, act):
        if condition is None:
            act()
        else:
            pl.when(condition)(act)

    def start(self):
        self.only(self.send_if, self.copy.start)

    def wait_send(self):
        self.only(self.send_if, self.copy.wait_send)

    def wait_recv(self):
        self.only(self.recv_if, self.copy.wait_recv)


def each(f, lo=0, hi=NB):
    def body(i, carry):
        f(i)
        return carry

    lax.fori_loop(lo, hi, body, 0)


def kernel(
    tokens, cot, lens, small_in, m_qkv, m_dense, m_in, m_out,
    block_out, tokens_grad, o_qkv, o_in, o_out, o_dense, o_small, *scratch,
):
    s = Holder()
    it = iter(scratch)
    for name in VMEM_SHAPES:
        setattr(s, name, next(it))
    sends = {name: next(it) for name in SEMS}
    recvs = {name: next(it) for name in SEMS}

    r, z, c = lax.axis_index("rep"), lax.axis_index("zero"), lax.axis_index("ctx")
    y, zl, x, core = z // 2, lax.rem(z, 2), c // 2, lax.rem(c, 2)

    def dev(rr, yy, ll, xx, kk):
        return (rr, yy * 2 + ll, xx * 2 + kk)

    def make(name, index, src, dst, target, send_if=None, recv_if=None):
        copy = pltpu.make_async_remote_copy(
            src_ref=src, dst_ref=dst, send_sem=sends[name].at[index], recv_sem=recvs[name].at[index],
            device_id=target, device_id_type=MESH)
        return Transfer(copy, send_if, recv_if)

    def start(transfers):
        for transfer in transfers:
            transfer.start()
        return transfers

    def wait_recv(transfers):
        for transfer in transfers:
            transfer.wait_recv()

    def wait_send(transfers):
        for transfer in transfers:
            transfer.wait_send()

    def y_at(d):
        return lax.rem(y + d, 4)

    def x_at(d):
        return lax.rem(x + d, 4)

    def z_at(d):
        place = lax.rem(2 * r + zl + d, 4)
        return place // 2, lax.rem(place, 2)

    def along_x(d):
        return dev(r, y, zl, x_at(d), core)

    def along_y(d):
        return dev(r, y_at(d), zl, x, core)

    def along_z(d):
        rr, ll = z_at(d)
        return dev(rr, y, ll, x, core)

    def block_of(xx, kk):
        return xx * 2 + kk

    sib = dev(r, y, zl, x, 1 - core)
    diagonal = z == c
    plane = zl == core
    finals = []

    loads = []

    def load(index, src, dst):
        copy = pltpu.make_async_copy(src, dst, sends["load"].at[index])
        copy.start()
        loads.append(copy)

    for t in range(3):
        load(t, m_qkv.at[:, part(c + 8 * t, 128)], s.dk.at[128 * t : 128 * t + 128, :])
    for t in range(3, 7):
        load(t, m_in.at[:, part((2 * (t - 3) + core) * 4 + x, 128)], s.dk.at[128 * t : 128 * t + 128, :])
    for t in range(8):
        load(7 + t, m_out.at[part(x, 128), 128 * t : 128 * t + 128], s.dv.at[128 * t : 128 * t + 128, :])
        load(15 + t, m_dense.at[:, 128 * t : 128 * t + 128], s.dv.at[D + 128 * t : D + 128 * t + 128, :])

    barrier = pltpu.get_barrier_semaphore()
    peers = [along_x(1), along_x(2), along_x(3), sib]
    for dr in range(2):
        for dy in range(4):
            for dl in range(2):
                if dr or dy or dl:
                    peers.append(dev(lax.rem(r + dr, 2), y_at(dy), lax.rem(zl + dl, 2), x, core))
    for p in peers:
        pl.semaphore_signal(barrier, inc=1, device_id=p, device_id_type=MESH)

    own, inverse = unit_norm(tokens[...].astype(F32))
    s.n[rows(c), :] = own.astype(BF)
    first, second = lens[0, 0], lens[0, 1]
    second_start = (first + BLOCK - 1) // BLOCK * BLOCK

    def masked_cotangent():
        place = lax.broadcasted_iota(jnp.int32, (R, D), 0) + c * R
        valid = (place < first) | ((place >= second_start) & (place < second_start + second))
        return jnp.where(valid, cot[...].astype(F32), 0.0)

    s.back[rows(c), :] = masked_cotangent().astype(BF)
    s.small[pl.ds(z, 1)] = jnp.zeros((1, 16, 128), F32)
    s.small[pl.ds(z, 1), 0:13] = small_in[...].astype(BF).astype(F32)[None]
    for t in range(7):
        loads[t].wait()
        s.w1r[part(z, 128), 128 * t : 128 * t + 128] = s.dk[128 * t : 128 * t + 128, :].astype(BF)
    pl.semaphore_wait(barrier, len(peers))

    lb, rb, ob = block_of(x_at(3), core), block_of(x_at(1), core), block_of(x_at(2), core)

    def gather(name, buf):
        def half(b, h):
            return buf.at[pl.ds(pl.multiple_of(b * R + 128 * h, 128), 128), :]

        def whole(b):
            return buf.at[rows(b), :]

        def same(index, ref, target):
            return make(name, index, ref, ref, target)

        return [
            same(0, half(c, 0), along_x(1)),
            same(1, half(c, 1), along_x(3)),
            same(2, half(c, 1), along_x(1)),
            same(3, half(c, 0), along_x(3)),
            same(4, whole(c), sib),
            same(5, half(lb, 0), along_x(1)),
            same(6, half(rb, 1), along_x(3)),
            same(7, whole(lb), sib),
            same(8, whole(rb), sib),
            same(9, whole(ob), sib),
        ]

    def gather_forward(g, steps):
        for got, sent in steps:
            g[got].wait_recv()
            g[sent].start()

    to_chips, to_sibs = ((0, 5), (1, 6)), ((2, 7), (3, 8))

    def gather_across(g):
        g[5].wait_recv()
        g[6].wait_recv()
        g[9].start()

    def gather_done(g):
        wait_recv([g[4], g[7], g[8], g[9]])

    n_gather = gather("n", s.n)
    start(n_gather[:5])

    def spread(name, buf, row, same_send=None, same_recv=None, cross_send=None, cross_recv=None):
        out = []
        whole = buf.at[pl.ds(pl.multiple_of(row, 128), 128), :]
        for dy in (1, 3, 2):
            recv_if = same_recv(dy) if same_recv else None
            out.append(make(name, dy - 1, whole, whole, along_y(dy), same_send, recv_if))
        for dy in (0, 1, 3, 2):
            for h in range(2):
                ref = buf.at[pl.ds(pl.multiple_of(row + 64 * h, 64), 64), :]
                target = dev(r if h == 0 else 1 - r, y_at(dy), 1 - zl, x, core)
                recv_if = cross_recv(dy) if cross_recv else None
                out.append(make(name, 3 + 2 * dy + h, ref, ref, target, cross_send, recv_if))
        return out

    small_gather = []
    for dy in range(4):
        for dl in range(2):
            if dy or dl:
                target = dev(r, y_at(dy), lax.rem(zl + dl, 2), x, core)
                small_gather.append(make("small", 2 * dy + dl - 1, s.small.at[z], s.small.at[z], target))
    start(small_gather)
    w1_near, w1_far = [], []
    for dy in range(4):
        row = (y_at(4 - dy) * 2 + zl) * 128
        if dy:
            ref = s.w1r.at[part(z, 128), :]
            w1_near.append(make("w1", dy - 1, ref, ref, along_y(dy)))
        for h in range(2):
            ref = s.w1r.at[pl.ds(pl.multiple_of(row + 64 * h, 64), 64), :]
            target = dev(r if h == 0 else 1 - r, y, 1 - zl, x, core)
            w1_far.append(make("w1", 3 + 2 * dy + h, ref, ref, target))
    start([w1_near[0], w1_near[2], w1_near[1]])
    start(w1_far[0:2])

    lane_place = lax.broadcasted_iota(jnp.int32, (8, T), 1)
    in_first = lane_place < first
    in_second = (lane_place >= second_start) & (lane_place < second_start + second)
    s.low[...] = jnp.where(in_first, 0, jnp.where(in_second, second_start, lane_place))
    position = jnp.where(in_first, lane_place, jnp.where(in_second, lane_place - second_start, 0))
    entry = lax.broadcasted_iota(jnp.int32, (8, T), 0)
    frequency = jnp.zeros((8, T), F32)
    for t in range(8):
        frequency = jnp.where(entry == t, 10000.0 ** (-t / 8), frequency)
    turn = position.astype(F32) * frequency
    s.angle[0:8, :] = jnp.cos(turn)
    s.angle[8:16, :] = jnp.sin(turn)

    def tables(b):
        cs, sn = s.angle[0:8, rows(b)], s.angle[8:16, rows(b)]
        rest = jnp.zeros((32, R), F32)
        s.turn[rows(b), :] = jnp.concatenate([cs, cs, sn, sn, rest] * 2, axis=0).T

    each(tables)
    s.flatG[...] = jnp.zeros_like(s.flatG)
    s.smallG[...] = jnp.zeros_like(s.smallG)

    gather_forward(n_gather, to_chips)
    for dy in (1, 3, 2):
        w1_near[dy - 1].wait_recv()
        start(w1_far[2 * dy : 2 * dy + 2])
    gather_forward(n_gather, to_sibs)
    back_gather = gather("back", s.back)
    start(back_gather[:5])

    for t in range(7, 23):
        loads[t].wait()
    wo_row = 128 + y * 128
    wo_spread = spread("wo", s.w2, wo_row, plane, lambda dy: plane, plane, lambda dy: zl != core)

    def dense_from(dy):
        return lax.rem(y + 4 - dy, 4) == x

    wd_spread = spread(
        "wd", s.w2, 0, diagonal, lambda dy: dense_from(dy) & plane, diagonal, lambda dy: dense_from(dy) & (zl != core))

    @pl.when(plane)
    def _():
        for t in range(8):
            cols = slice(128 * t, 128 * t + 128)
            s.w2[pl.ds(pl.multiple_of(wo_row, 128), 128), cols] = s.dv[128 * t : 128 * t + 128, :].astype(BF)

    @pl.when(diagonal)
    def _():
        for t in range(8):
            s.w2[0:128, 128 * t : 128 * t + 128] = s.dv[D + 128 * t : D + 128 * t + 128, :].astype(BF)

    s.dk[...] = jnp.zeros_like(s.dk)
    s.dv[...] = jnp.zeros_like(s.dv)
    s.dqT[...] = jnp.zeros_like(s.dqT)
    start(wd_spread)
    start(wo_spread)

    wait_recv(small_gather)
    for t in range(8):
        s.flat[13 * t : 13 * t + 13, :] = s.small[t, 0:13, :]
    s.cols[...] = s.flat[0:32, :].T
    wait_recv(w1_far)

    def line(at):
        return jnp.concatenate([s.flat[at + t : at + t + 1, :] for t in range(8)], axis=1)

    shifts = jnp.concatenate([line(8), line(24), jnp.zeros((6, D), F32)], axis=0).astype(BF)
    turned = nn(shifts, s.w1r[...])
    for t in range(3):
        cols = slice(128 * t, 128 * t + 128)
        s.bias[0:1, cols] = turned[0:1, cols] + s.flat[pl.ds(32 + 8 * t + c, 1), :]
    for t in range(4):
        cols = slice(QKV + 128 * t, QKV + 128 * t + 128)
        s.bias[0:1, cols] = turned[1:2, cols] + s.flat[pl.ds(72 + (2 * t + core) * 4 + x, 1), :]
    for t in range(8):
        sl = slice(128 * t, 128 * t + 128)
        s.w1[sl, :QKV] = (s.w1r[sl, :QKV].astype(F32) * s.cols[:, t : t + 1]).astype(BF)
        s.w1[sl, QKV:] = (s.w1r[sl, QKV:].astype(F32) * s.cols[:, 16 + t : 17 + t]).astype(BF)

    wait_recv(n_gather[4:5])

    def project_turn(t):
        p, q = t // 2, lax.rem(t, 2)

        @pl.when(t == 4)
        def _():
            gather_across(n_gather)
            wait_recv(n_gather[7:9])

        @pl.when(t == 6)
        def _():
            wait_recv(n_gather[9:])

        middle = lax.rem((p + 1) // 2, 2)
        dx = middle * (3 - 2 * q) + (1 - middle) * 2 * (p // 3)
        dk = middle * (p - 1) + (1 - middle) * q
        project(block_of(x_at(dx), lax.rem(core + dk, 2)), s)

    each(project_turn)
    gather_forward(back_gather, to_chips)

    class Owner:
        def __init__(self, buf, kind):
            self.buf, self.kind = buf, kind
            self.sib_slots, self.near_slots = getattr(s, "sib" + kind), getattr(s, "near" + kind)

        def to_sibling(self, xx):
            return make("sib" + self.kind, xx, self.buf.at[rows(block_of(xx, 1 - core)), :], self.sib_slots.at[xx], sib)

        def near(self, xx, d):
            return make(
                "near" + self.kind, d - 1, self.buf.at[rows(block_of(xx, core)), :], self.near_slots.at[d - 1],
                dev(r, y, zl, xx, core))

        def add(self, xx):
            self.to_sibling(xx).wait_recv()
            here = rows(block_of(xx, core))
            mine = self.buf[here, :].astype(F32) + self.sib_slots[pl.ds(xx, 1)][0].astype(F32)
            self.buf[here, :] = mine.astype(BF)
            pl.when(xx != x)(lambda: self.near(xx, lax.rem(x + 4 - xx, 4)).start())

        def total(self):
            total = self.buf[rows(c), :].astype(F32)
            for d in (1, 3, 2):
                self.near(x_at(4 - d), d).wait_recv()
                total = total + self.near_slots[d - 1].astype(F32)
            return total

        def drain(self):
            for xx in range(4):
                self.to_sibling(xx).wait_send()
            for d in (1, 2, 3):
                self.near(x_at(4 - d), d).wait_send()

    out_owner = Owner(s.n, "O")
    e_owner = Owner(s.back, "E")

    def down(i):
        s.n[rows(i), :] = nn(s.A[rows(i), :], s.w2[...]).astype(BF)

    def attend_turn(i):
        pl.when(i == 2)(lambda: gather_forward(back_gather, to_sibs))
        attend(i, s)

    def down_first(xx):
        down(block_of(xx, 1 - core))
        out_owner.to_sibling(xx).start()

    each(attend_turn, 0, 4)
    gather_across(back_gather)
    wait_send(n_gather)
    wait_recv(wd_spread)
    wait_recv(wo_spread)
    each(down_first, 0, 4)
    each(lambda xx: down(block_of(xx, core)), 0, 4)
    gather_done(back_gather)
    each(lambda b: pull_down(b, s), 0, 4)
    each(out_owner.add, 0, 4)
    each(lambda b: pull_down(b, s), 4, 8)

    def grad_down(t):
        cols = part(t, 256)
        g = nn(s.AT[...], s.back[:, cols]).astype(BF)
        for h in range(2):
            s.gd[h, :, cols] = g[64 * h : 64 * h + 64]
            for yy in range(4):
                s.go[yy, h, :, cols] = g[128 + 128 * yy + 64 * h : 192 + 128 * yy + 64 * h]

    each(grad_down, 0, 4)

    def down_grads_out():
        out = [make("yo", d - 1, s.go.at[y_at(d)], s.yo.at[d - 1], along_y(d)) for d in (1, 3, 2)]
        for d in (1, 3, 2):
            rr, ll = z_at(d)
            out.append(make("zd", d - 1, s.gd.at[rr], s.zd.at[d - 1], along_z(d), ll == core, plane))
        return out

    down_sends = start(down_grads_out())

    def z_sends(name, src, slots):
        return [make(name, d - 1, src.at[2 * z_at(d)[0] + z_at(d)[1]], slots.at[d - 1], along_z(d)) for d in (1, 3, 2)]

    def y_sends(name, src, slots):
        return [make(name, d - 1, src.at[y_at(d)], slots.at[d - 1], along_y(d)) for d in (1, 3, 2)]

    def z_sum(transfers, src, slots, out):
        wait_recv(transfers)
        mine = src[pl.ds(2 * r + zl, 1)][0].astype(F32)
        for d in range(3):
            mine = mine + slots[d].astype(F32)
        out[...] = mine.astype(out.dtype)

    def y_sum(transfers, src, slots):
        wait_recv(transfers)
        mine = src[pl.ds(y, 1)][0].astype(F32)
        for d in range(3):
            mine = mine + slots[d].astype(F32)
        return mine

    def grad_up(lo, hi, place, gain_at, shift_at):
        g = nn(s.nT[...], s.dP[:, lo:hi])
        total = jnp.sum(s.dP[:, lo:hi].astype(F32), axis=0, keepdims=True)
        for t in range(8):
            sl = slice(128 * t, 128 * t + 128)
            full = g[sl] * s.cols[:, gain_at + t : gain_at + t + 1] + s.cols[:, shift_at + t : shift_at + t + 1] * total
            for h in range(2):
                place(2 * h + t % 2, t // 2, full[64 * h : 64 * h + 64].astype(BF))
        return g, total

    def norm_sums(lo, hi, g, total):
        gains, moves = [], []
        for t in range(8):
            sl = slice(128 * t, 128 * t + 128)
            w = s.w1r[sl, lo:hi].astype(F32)
            gains.append(jnp.sum(w * g[sl], axis=1, keepdims=True))
            moves.append(jnp.sum(w * total, axis=1, keepdims=True))
        return jnp.concatenate(gains, axis=1), jnp.concatenate(moves, axis=1)

    def place_in(at):
        def place(p4, yy, value):
            s.gi[p4, yy, :, at : at + 256] = value

        return place

    def place_q(p4, yy, value):
        s.gq[p4, yy] = value

    def place_v(p4, yy, value):
        s.gv[yy, p4] = value

    g_a, total_a = grad_up(QKV, QKV + 256, place_in(0), 16, 24)
    g_b, total_b = grad_up(QKV + 256, WIDE, place_in(256), 16, 24)
    zi_sends = start(z_sends("zi", s.gi, s.zi))
    gain_a, move_a = norm_sums(QKV, QKV + 256, g_a, total_a)
    gain_b, move_b = norm_sums(QKV + 256, WIDE, g_b, total_b)
    s.flatG[16:32, :] = jnp.concatenate([gain_a + gain_b, move_a + move_b], axis=1).T
    for t in range(4):
        total = total_a if t < 2 else total_b
        at = 128 * (t % 2)
        s.flatG[pl.ds(72 + (2 * t + core) * 4 + x, 1), :] = total[:, at : at + 128]
    back_sum = jnp.sum(s.back[rows(c), :].astype(F32), axis=0, keepdims=True)
    for t in range(8):
        s.flatG[56 + t : 57 + t, :] = back_sum[:, 128 * t : 128 * t + 128]
        s.flatG[64 + t : 65 + t, :] = back_sum[:, 128 * t : 128 * t + 128]

    wait_send(back_gather)

    def turn_x(t):
        return 3 - lax.rem(t, 4)

    def turn_core(t):
        return lax.rem(turn_x(t) + t // 4, 2)

    def back_sum(t):
        @pl.when(turn_core(t) == core)
        def _():
            e_owner.add(turn_x(t))

    def back_step(t):
        b = block_of(turn_x(t), turn_core(t))
        late = t // 4
        row_pairs = (4 - t) * (1 - late) + (4 - t // 2) * late
        column_pairs = ((t + 1) // 2) * (1 - late)
        each(lambda l: tile_back(b, R, late + (2 + 2 * late) * l, PAIR, s), 0, row_pairs)
        each(lambda l: tile_back(5 - 4 * (column_pairs - 1) + 4 * l, PAIR, b, R, s), 0, column_pairs)
        finish_back(b, s)

        @pl.when(turn_core(t) != core)
        def _():
            e_owner.to_sibling(turn_x(t)).start()

        pl.when(t > 0)(lambda: back_sum(t - 1))

    def final_gather(name, buf, out, slot, source=None):
        def has(xx, kk):
            return source(xx, kk) if source else None

        def at(xx, kk):
            return slot(out, xx, kk)

        local = pltpu.make_async_copy(buf, at(x, core), sends[name].at[7])
        first_hop = [
            make(name, d - 1, buf, at(x, core), along_x(d), has(x, core), has(x_at(4 - d), core)) for d in (1, 3, 2)]
        first_hop.append(make(name, 3, buf, at(x, core), sib, has(x, core), has(x, 1 - core)))
        second_hop = []
        for d in (1, 3, 2):
            xx = x_at(4 - d)
            ref = at(xx, core)
            second_hop.append(make(name, 3 + d, ref, ref, sib, has(xx, core), has(xx, 1 - core)))
        return Transfer(local, has(x, core)), first_hop, second_hop

    def final_start(g):
        g[0].start()
        start(g[1])

    def final_forward(g):
        own_copy, first_hop, second_hop = g
        for got, sent in zip(first_hop[:3], second_hop):
            got.wait_recv()
            sent.start()

    def final_finish(g):
        own_copy, first_hop, second_hop = g
        own_copy.only(own_copy.send_if, own_copy.copy.wait)
        first_hop[3].wait_recv()
        wait_recv(second_hop)
        finals.extend(first_hop + second_hop)

    yi_sends = y_sends("yi", s.ti, s.yi)
    second_sends = []
    for d in (1, 3, 2):
        rr, ll = z_at(d)
        second_sends.append(make("zo", d - 1, s.to.at[rr], s.zo.at[d - 1], along_z(d), ll == core, plane))

    def to_diagonal(d):
        return make("yd", d - 1, s.td, s.yd.at[d - 1], along_y(d), plane & (y_at(d) == x), diagonal)

    second_dense = [to_diagonal(d) for d in (1, 3, 2)]

    def early_second():
        z_sum(zi_sends, s.gi, s.zi, s.ti)
        start(yi_sends)
        wait_recv(down_sends)
        total = s.go[pl.ds(y, 1)][0].astype(F32) + s.yo[0].astype(F32) + s.yo[1].astype(F32) + s.yo[2].astype(F32)
        s.to[...] = total.astype(BF)

        @pl.when(plane)
        def _():
            mine = s.gd[pl.ds(r, 1)][0].astype(F32)
            for d in range(3):
                mine = mine + s.zd[d].astype(F32)
            s.td[...] = mine.astype(BF)

        start(second_sends)
        start(second_dense)

    other = dev(1 - r, y, zl, x, core)

    def halves(name, buf, condition=None):
        ref = buf.at[r] if len(buf.shape) == 3 else buf.at[:, r]
        return make(name, 0, ref, ref, other, condition, condition)

    def in_blocks(value, buf):
        for t in range(buf.shape[0]):
            buf[t, pl.ds(r, 1)] = value[:, 128 * t : 128 * t + 128].astype(BF)[None]

    early = [halves("ri", s.fi), halves("ro", s.fo, plane), halves("rd", s.fd, diagonal)]

    def early_whole():
        in_blocks(y_sum(yi_sends, s.ti, s.yi), s.fi)
        wait_recv(second_sends)
        wait_recv(second_dense)

        @pl.when(plane)
        def _():
            mine = s.to[pl.ds(r, 1)][0].astype(F32)
            for d in range(3):
                mine = mine + s.zo[d].astype(F32)
            s.fo[pl.ds(r, 1)] = mine.astype(BF)[None]

        @pl.when(diagonal)
        def _():
            mine = s.td[...].astype(F32)
            for d in range(3):
                mine = mine + s.yd[d].astype(F32)
            s.fd[pl.ds(r, 1)] = mine.astype(BF)[None]
        start(early)

    g_in = final_gather("ai", s.fi, o_in, lambda out, xx, kk: out.at[:, kk, xx])
    g_out = final_gather("ao", s.fo, o_out, lambda out, xx, kk: out.at[xx], lambda xx, kk: zl == kk)
    g_dense = final_gather("ad", s.fd, o_dense, lambda out, xx, kk: out, lambda xx, kk: (zl == kk) & (y == xx))

    def early_gather():
        wait_recv(early)
        for g in (g_in, g_out, g_dense):
            final_start(g)

    def back_turn(t):
        back_step(t)
        pl.when(t == EARLY_SECOND)(early_second)
        pl.when(t == EARLY_WHOLE)(early_whole)
        pl.when(t == EARLY_GATHER)(early_gather)

    each(back_turn)
    back_sum(7)
    g_q, total_q = grad_up(0, 256, place_q, 0, 8)
    zq_sends = start(z_sends("zq", s.gq, s.zq))
    g_v, total_v = grad_up(256, QKV, place_v, 0, 8)
    yv_sends = start(y_sends("yv", s.gv, s.yv))
    gain_q, move_q = norm_sums(0, 256, g_q, total_q)
    gain_v, move_v = norm_sums(256, QKV, g_v, total_v)
    s.flatG[0:16, :] = jnp.concatenate([gain_q + gain_v, move_q + move_v], axis=1).T
    s.flatG[pl.ds(32 + c, 1), :] = total_q[:, 0:128]
    s.flatG[pl.ds(40 + c, 1), :] = total_q[:, 128:256]
    s.flatG[pl.ds(48 + c, 1), :] = total_v
    for t in range(8):
        s.smallG[t % 2, t // 2, 0:13, :] = s.flatG[13 * t : 13 * t + 13, :]
    small_z = start([make("smallZ", d - 1, s.smallG.at[z_at(d)[1]], s.smallZ.at[d - 1], along_z(d)) for d in (1, 3, 2)])

    total = out_owner.total()
    bias = jnp.concatenate([s.flat[56 + t : 57 + t, :] + s.flat[64 + t : 65 + t, :] for t in range(8)], axis=1)
    block_out[...] = (tokens[...].astype(F32) + bias + total).astype(BF)

    s.tv[...] = y_sum(yv_sends, s.gv, s.yv).astype(BF)
    zv_sends = start(z_sends("zv", s.tv, s.zv))
    z_sum(zq_sends, s.gq, s.zq, s.tq)
    yq_sends = start(y_sends("yq", s.tq, s.yq))
    wait_recv(small_z)
    s.smallT[...] = s.smallG[pl.ds(zl, 1)][0] + s.smallZ[0] + s.smallZ[1] + s.smallZ[2]
    small_y = start(y_sends("smallY", s.smallT, s.smallY))
    wait_recv(zv_sends)
    mine = s.tv[pl.ds(2 * r + zl, 1)][0].astype(F32)
    for d in range(3):
        mine = mine + s.zv[d].astype(F32)
    in_blocks(jnp.concatenate([y_sum(yq_sends, s.tq, s.yq), mine], axis=1), s.fq)
    late = start([halves("rq", s.fq)])
    s.smallU[...] = y_sum(small_y, s.smallT, s.smallY)
    small_x = start([make("smallX", d - 1, s.smallU, s.smallX.at[d - 1], along_x(d)) for d in (1, 3, 2)])

    wait_recv(late)
    g_qkv = final_gather("aq", s.fq, o_qkv, lambda out, xx, kk: out.at[:, block_of(xx, kk)])
    final_start(g_qkv)
    final_forward(g_in)
    final_forward(g_out)
    final_forward(g_dense)

    e = e_owner.total()
    own, inverse = unit_norm(tokens[...].astype(F32))
    mean_e = jnp.mean(e, axis=-1, keepdims=True)
    mean_en = jnp.mean(e * own, axis=-1, keepdims=True)
    tokens_grad[...] = masked_cotangent() + inverse * (e - mean_e - own * mean_en)

    wait_recv(small_x)
    s.smallV[...] = s.smallU[...] + s.smallX[0] + s.smallX[1] + s.smallX[2]
    small_s = start([make("smallS", 0, s.smallV, s.smallS, sib)])
    final_forward(g_qkv)
    wait_recv(small_s)
    o_small[...] = s.smallV[...] + s.smallS[...]

    for g in (g_in, g_out, g_dense, g_qkv):
        final_finish(g)
    out_owner.drain()
    e_owner.drain()
    for group in (
        finals, small_gather, w1_near, w1_far, wo_spread, wd_spread, down_sends, zi_sends, yi_sends, second_sends, second_dense,
        early, zq_sends, yq_sends, yv_sends, zv_sends, late, small_z, small_y, small_x, small_s,
    ):
        wait_send(group)


def block_step(tokens, cot, lens, small_in, m_qkv, m_dense, m_in, m_out):
    vmem = pl.BlockSpec(memory_space=pltpu.VMEM)
    hbm = pl.BlockSpec(memory_space=pl.ANY)
    shapes = [
        jax.ShapeDtypeStruct((R, D), BF), jax.ShapeDtypeStruct((R, D), F32),
        jax.ShapeDtypeStruct((3, 8, 2, 64, 128), BF), jax.ShapeDtypeStruct((4, 2, 4, 2, 64, 128), BF),
        jax.ShapeDtypeStruct((4, 2, 64, D), BF), jax.ShapeDtypeStruct((2, 64, D), BF),
        jax.ShapeDtypeStruct((16, 128), F32),
    ]
    scratch = [pltpu.VMEM(shape, kind) for shape, kind in VMEM_SHAPES.values()]
    scratch += [pltpu.SemaphoreType.DMA((count,)) for count in SEMS.values()] * 2
    return pl.pallas_call(
        kernel,
        out_shape=shapes,
        in_specs=[vmem, vmem, pl.BlockSpec(memory_space=pltpu.SMEM), vmem, hbm, hbm, hbm, hbm],
        out_specs=[vmem, vmem, hbm, hbm, hbm, hbm, vmem],
        scratch_shapes=scratch,
        compiler_params=pltpu.CompilerParams(
            collective_id=0, has_side_effects=True, vmem_limit_bytes=VMEM_LIMIT),
        name="block_step",
    )(tokens, cot, lens, small_in, m_qkv, m_dense, m_in, m_out)


VMEM_LIMIT = 60 * 2**20


def adam_update(master, first_old, second_old, gradient, rate):
    first_new = BETA_ONE * first_old + (1.0 - BETA_ONE) * gradient
    second_new = BETA_TWO * second_old + (1.0 - BETA_TWO) * gradient * gradient
    first_hat = first_new / (1.0 - BETA_ONE**STEP)
    second_hat = second_new / (1.0 - BETA_TWO**STEP)
    updated = master - rate * (first_hat / (jnp.sqrt(second_hat) + ADAM_EPS) + DECAY * master)
    return gradient, second_new, updated


def adam_chunks():
    cols = [(0, b, 6) for b in range(0, 24, 6)] + [(2, b, 8) for b in range(0, 32, 8)]
    out = [(t, (slice(None), slice(128 * b, 128 * (b + n))), slice(b, b + n)) for t, b, n in cols]
    out += [(3, slice(128 * b, 128 * b + 128), slice(128 * b, 128 * b + 128)) for b in range(4)]
    return out + [(1, slice(None), slice(None)), (4, slice(None), slice(0, 13))]


def adam_kernel(*refs):
    grads, state, given, outs, passed = refs[:5], refs[5:20], refs[20:22], refs[22:37], refs[37:39]
    grad_vmem, state_vmem, given_vmem = refs[39:44], refs[44:59], refs[59:61]
    in_sem, out_sem, given_sem, passed_sem = refs[61:65]
    chunks = adam_chunks()
    loads, stores = [], []
    for n, (t, at, grad_at) in enumerate(chunks):
        group = [pltpu.make_async_copy(grads[t].at[grad_at], grad_vmem[t].at[grad_at], in_sem.at[n, 3])]
        for o in range(3):
            k = 5 * o + t
            group.append(pltpu.make_async_copy(state[k].at[at], state_vmem[k].at[at], in_sem.at[n, o]))
        for copy in group:
            copy.start()
        loads.append(group)
    givens = [pltpu.make_async_copy(given[n], given_vmem[n], given_sem.at[n]) for n in range(2)]
    for copy in givens:
        copy.start()
    for n, (t, at, grad_at) in enumerate(chunks):
        for copy in loads[n]:
            copy.wait()
        bufs = [state_vmem[5 * o + t] for o in range(3)]

        def step(where, gradient, t=t, bufs=bufs):
            master, first, second = (buf[where] for buf in bufs)
            _, renewed, updated = adam_update(master, first, second, gradient, RATES[t])
            bufs[0][where], bufs[1][where], bufs[2][where] = updated, gradient, renewed

        if t in (0, 2):
            for b in range(grad_at.start, grad_at.stop):
                step((slice(None), slice(128 * b, 128 * b + 128)), grad_vmem[t][b].astype(F32))
        else:
            step((at, slice(None)), grad_vmem[t][grad_at, :].astype(F32))
        for o, buf in ((0, bufs[1]), (1, bufs[2]), (2, bufs[0])):
            copy = pltpu.make_async_copy(buf.at[at], outs[5 * o + t].at[at], out_sem.at[n, o])
            copy.start()
            stores.append(copy)
    for n in range(2):
        givens[n].wait()
        copy = pltpu.make_async_copy(given_vmem[n], passed[n], passed_sem.at[n])
        copy.start()
        stores.append(copy)
    for copy in stores:
        copy.wait()


def adam_step(grads, state, given):
    hbm = pl.BlockSpec(memory_space=pl.ANY)
    count = len(adam_chunks())
    return pl.pallas_call(
        adam_kernel,
        out_shape=[jax.ShapeDtypeStruct(a.shape, a.dtype) for a in (*state, *given)],
        in_specs=[hbm] * 22,
        out_specs=[hbm] * 17,
        scratch_shapes=[pltpu.VMEM(a.shape, a.dtype) for a in (*grads, *state, *given)]
        + [pltpu.SemaphoreType.DMA(shape) for shape in ((count, 4), (count, 3), (2,), (2,))],
        compiler_params=pltpu.CompilerParams(vmem_limit_bytes=VMEM_LIMIT),
        name="adam_step",
    )(*grads, *state, *given)


def per_device(tokens, cotangent, seq_lengths, *state):
    state = [a.reshape(13, 128) if a.ndim == 1 else a for a in state]
    block_out, tokens_grad, g_qkv, g_in, g_out, g_dense, g_small = block_step(
        tokens, cotangent, seq_lengths, state[4], *state[:4])
    grads = [
        g_qkv.reshape(24, 128, 128), g_dense.reshape(128, D), g_in.reshape(32, 128, 128), g_out.reshape(512, D), g_small]
    *results, block_out, tokens_grad = adam_step(grads, state, [block_out, tokens_grad])
    return (block_out, tokens_grad, *(a.reshape(-1) if a.shape[0] == 13 else a for a in results))


def solution(mesh):
    seq = P(("rep", "zero", "ctx"), None)
    state = (P("zero", None),) * 4 + (P("zero"),)
    return jax.shard_map(
        per_device,
        mesh=mesh,
        in_specs=(seq, seq, P(("rep", "zero"), None)) + state * 3,
        out_specs=(seq, seq) + state * 3,
        check_vma=False,
    )
```

```python
import functools
import math

import jax
import jax.numpy as jnp
from jax import lax
from jax.experimental import pallas as pl
from jax.experimental.pallas import tpu as pltpu
from jax.sharding import PartitionSpec as P

D = 1024
T = 2048
R = 256
NB = 8
BLOCK = 128
PAIR = 2 * R
EARLY_SECOND = 3
EARLY_WHOLE = 6
EARLY_GATHER = 7
STEP = 10
QKV = 384
UP = 512
WIDE = QKV + UP
DOWN = 640
EPSILON = 1e-05
BETA_ONE = 0.9
BETA_TWO = 0.999
ADAM_EPS = 1e-08
DECAY = 0.01
RATES = (0.25, 1.0, 0.25, 0.2, 0.5)
NEG = -1e30
BF = jnp.bfloat16
F32 = jnp.float32
MESH = pl.DeviceIdType.MESH


def nn(a, b):
    return lax.dot_general(a, b, (((1,), (0,)), ((), ())), preferred_element_type=F32)


def nt(a, b):
    return lax.dot_general(a, b, (((1,), (1,)), ((), ())), preferred_element_type=F32)


def rows(block):
    return pl.ds(pl.multiple_of(block * R, R), R)


def span(start, size):
    return pl.ds(pl.multiple_of(start * R, R), size)


def part(index, size):
    return pl.ds(pl.multiple_of(index * size, size), size)


def turns(table):
    lane = lax.broadcasted_iota(jnp.int32, table.shape, 1) % 64
    return jnp.where(lane < 16, table, 1.0), jnp.where(lane < 16, pltpu.roll(table, 112, 1), 0.0)


def rope(u, cosine, sine, sign):
    lane = lax.broadcasted_iota(jnp.int32, u.shape, 1) % 64
    above = pltpu.roll(u, 8, 1)
    below = pltpu.roll(u, u.shape[1] - 8, 1)
    return u * cosine + (sign * jnp.where(lane < 8, -below, above)) * sine


def head_mask(x, head):
    lane = lax.broadcasted_iota(jnp.int32, x.shape, 1)
    return jnp.where((lane >= 64 * head) & (lane < 64 * head + 64), x, jnp.zeros_like(x))


def project(b, s):
    nb = s.n[rows(b), :]
    s.nT[:, rows(b)] = nb.T
    h = nn(nb, s.w1[:, :QKV]) + s.bias[0:1, :QKV]
    cosine, sine = turns(s.turn[rows(b), :])
    s.q[rows(b), :] = (rope(h[:, :128], cosine, sine, 1.0) * 0.125).astype(BF)
    kb = rope(h[:, 128:256], cosine, sine, 1.0).astype(BF)
    vb = h[:, 256:384].astype(BF)
    s.k[rows(b), :] = kb
    s.kT[:, rows(b)] = kb.T
    s.v[rows(b), :] = vb
    s.vT[:, rows(b)] = vb.T
    for t in range(2):
        cols = slice(QKV + 256 * t, QKV + 256 * t + 256)
        hid = slice(128 + 256 * t, 384 + 256 * t)
        x = nn(nb, s.w1[:, cols]) + s.bias[0:1, cols]
        cdf = 0.5 + 0.5 * lax.erf(x * (1 / math.sqrt(2)))
        pdf = jnp.exp(-0.5 * x * x) * (1 / math.sqrt(2 * math.pi))
        act = (x * cdf).astype(BF)
        s.dP[rows(b), cols] = (cdf + x * pdf).astype(BF)
        s.A[rows(b), hid] = act
        s.AT[hid, rows(b)] = act.T


def attend(i, s):
    here = part(i, PAIR)
    qb = s.q[here, :]
    low = s.low[0:1, here]
    heads = [head_mask(qb, h) for h in range(2)]

    def block(j, carry, diagonal=False):
        there = part(j, PAIR)
        key = lax.broadcasted_iota(jnp.int32, (PAIR, PAIR), 0)
        seen = key >= low - j * PAIR
        if diagonal:
            seen = seen & (key <= lax.broadcasted_iota(jnp.int32, (PAIR, PAIR), 1))
        kb = s.k[there, :]
        scores = [jnp.where(seen, nt(kb, heads[h]), NEG) for h in range(2)]
        out = []
        for h in range(2):
            top, total, o = carry[h]
            new = jnp.maximum(top, jnp.max(scores[h], axis=0, keepdims=True))
            p = jnp.exp(scores[h] - new)
            scale = jnp.exp(top - new)
            total = total * scale + jnp.sum(p, axis=0, keepdims=True)
            out.append((new, total, o * scale + nn(s.vT[64 * h : 64 * h + 64, there], p.astype(BF))))
        return tuple(out)

    start = (jnp.full((1, PAIR), NEG, F32), jnp.zeros((1, PAIR), F32), jnp.zeros((64, PAIR), F32))
    carry = lax.fori_loop(0, i, block, block(i, (start, start), True))
    oT = jnp.concatenate([o / total for top, total, o in carry], axis=0).astype(BF)
    s.AT[0:128, here] = oT
    s.A[here, 0:128] = oT.T
    for h in range(2):
        s.lse[h : h + 1, here] = carry[h][0] + jnp.log(carry[h][1])


def pull_down(b, s):
    bb = s.back[rows(b), :]
    d = nt(bb, s.w2[0:128, :]).astype(BF)
    s.dO[rows(b), :] = d
    w = d.astype(F32).T * s.AT[0:128, rows(b)].astype(F32)
    for h in range(2):
        s.lse[2 + h : 3 + h, rows(b)] = jnp.sum(w[64 * h : 64 * h + 64], axis=0, keepdims=True)
    for t in range(2):
        cols = slice(QKV + 256 * t, QKV + 256 * t + 256)
        d = nt(bb, s.w2[128 + 256 * t : 384 + 256 * t, :])
        s.dP[rows(b), cols] = (d * s.dP[rows(b), cols].astype(F32)).astype(BF)


def tile_back(first_query, queries, first_key, keys, s):
    qs, ks = span(first_query, queries), span(first_key, keys)
    qb, db = s.q[qs, :], s.dO[qs, :]
    kb, vb = s.k[ks, :], s.v[ks, :]
    key = lax.broadcasted_iota(jnp.int32, (keys, queries), 0)
    query = lax.broadcasted_iota(jnp.int32, (keys, queries), 1)
    seen = (key >= s.low[0:1, qs] - first_key * R) & (key <= query + (first_query - first_key) * R)
    dk, dv = 0.0, 0.0
    for h in range(2):
        qh, dh = head_mask(qb, h), head_mask(db, h)
        p = jnp.where(seen, jnp.exp(nt(kb, qh) - s.lse[h : h + 1, qs]), 0.0)
        ds = (p * (nt(vb, dh) - s.lse[2 + h : 3 + h, qs])).astype(BF)
        dv = dv + nn(p.astype(BF), dh)
        dk = dk + nn(ds, qh)
        s.dqT[64 * h : 64 * h + 64, qs] += nn(s.kT[64 * h : 64 * h + 64, ks], ds)
    s.dv[ks, :] += dv
    s.dk[ks, :] += dk


def finish_back(b, s):
    cosine, sine = turns(s.turn[rows(b), :])
    s.dP[rows(b), 0:128] = rope(s.dqT[:, rows(b)].T * 0.125, cosine, sine, -1.0).astype(BF)
    s.dP[rows(b), 128:256] = rope(s.dk[rows(b), :], cosine, sine, -1.0).astype(BF)
    s.dP[rows(b), 256:384] = s.dv[rows(b), :].astype(BF)
    s.back[rows(b), :] = nt(s.dP[rows(b), :], s.w1[...]).astype(BF)


def unit_norm(x):
    mean = jnp.mean(x, axis=-1, keepdims=True)
    centered = x - mean
    var = jnp.mean(centered * centered, axis=-1, keepdims=True)
    inv = lax.rsqrt(var + EPSILON)
    return centered * inv, inv


VMEM_SHAPES = dict(
    n=((T, D), BF), nT=((D, T), BF), back=((T, D), BF),
    w1r=((D, WIDE), BF), w1=((D, WIDE), BF), w2=((DOWN, D), BF),
    q=((T, 128), BF), k=((T, 128), BF), v=((T, 128), BF), kT=((128, T), BF), vT=((128, T), BF),
    A=((T, DOWN), BF), AT=((DOWN, T), BF), dP=((T, WIDE), BF), dO=((T, 128), BF),
    dk=((T, 128), F32), dqT=((128, T), F32), dv=((T, 128), F32), lse=((8, T), F32), low=((8, T), jnp.int32),
    angle=((16, T), F32), turn=((T, 128), F32),
    bias=((8, WIDE), F32), flat=((104, 128), F32), cols=((128, 32), F32),
    sibO=((4, R, D), BF), nearO=((3, R, D), BF), sibE=((4, R, D), BF), nearE=((3, R, D), BF),
    small=((8, 16, 128), F32), flatG=((104, 128), F32), smallG=((2, 4, 16, 128), F32), smallZ=((3, 4, 16, 128), F32),
    smallT=((4, 16, 128), F32), smallY=((3, 16, 128), F32), smallU=((16, 128), F32), smallX=((3, 16, 128), F32),
    smallV=((16, 128), F32), smallS=((16, 128), F32),
    gi=((4, 4, 64, UP), BF), gq=((4, 4, 64, 256), BF), gv=((4, 4, 64, 128), BF), gd=((2, 64, D), BF), go=((4, 2, 64, D), BF),
    zi=((3, 4, 64, UP), BF), zq=((3, 4, 64, 256), BF), yv=((3, 4, 64, 128), BF), zd=((3, 64, D), BF), yo=((3, 2, 64, D), BF),
    ti=((4, 64, UP), BF), tq=((4, 64, 256), BF), tv=((4, 64, 128), BF), td=((64, D), BF), to=((2, 64, D), BF),
    yi=((3, 64, UP), BF), yq=((3, 64, 256), BF), zv=((3, 64, 128), BF), yd=((3, 64, D), BF), zo=((3, 64, D), BF),
    fi=((4, 2, 64, 128), BF), fq=((3, 2, 64, 128), BF), fd=((2, 64, D), BF), fo=((2, 64, D), BF),
)
SEMS = dict(
    load=23, n=10, back=10, w1=11, wo=11, wd=11, small=7,
    sibO=4, nearO=3, sibE=4, nearE=3, zi=3, zq=3, yv=3, zv=3, zd=3, yo=3, yi=3, yq=3, yd=3, zo=3,
    smallZ=3, smallY=3, smallX=3, smallS=1,
    ri=1, rq=1, rd=1, ro=1, ai=9, aq=9, ao=9, ad=9,
)


class Holder:
    pass


class Transfer:
    def __init__(self, copy, send_if=None, recv_if=None):
        self.copy, self.send_if, self.recv_if = copy, send_if, recv_if

    def only(self, condition, act):
        if condition is None:
            act()
        else:
            pl.when(condition)(act)

    def start(self):
        self.only(self.send_if, self.copy.start)

    def wait_send(self):
        self.only(self.send_if, self.copy.wait_send)

    def wait_recv(self):
        self.only(self.recv_if, self.copy.wait_recv)


def each(f, lo=0, hi=NB):
    def body(i, carry):
        f(i)
        return carry

    lax.fori_loop(lo, hi, body, 0)


def kernel(
    tokens, cot, lens, small_in, m_qkv, m_dense, m_in, m_out,
    block_out, tokens_grad, o_qkv, o_in, o_out, o_dense, o_small, *scratch,
):
    s = Holder()
    it = iter(scratch)
    for name in VMEM_SHAPES:
        setattr(s, name, next(it))
    sends = {name: next(it) for name in SEMS}
    recvs = {name: next(it) for name in SEMS}

    r, z, c = lax.axis_index("rep"), lax.axis_index("zero"), lax.axis_index("ctx")
    y, zl, x, core = z // 2, lax.rem(z, 2), c // 2, lax.rem(c, 2)

    def dev(rr, yy, ll, xx, kk):
        return (rr, yy * 2 + ll, xx * 2 + kk)

    def make(name, index, src, dst, target, send_if=None, recv_if=None):
        copy = pltpu.make_async_remote_copy(
            src_ref=src, dst_ref=dst, send_sem=sends[name].at[index], recv_sem=recvs[name].at[index],
            device_id=target, device_id_type=MESH)
        return Transfer(copy, send_if, recv_if)

    def start(transfers):
        for transfer in transfers:
            transfer.start()
        return transfers

    def wait_recv(transfers):
        for transfer in transfers:
            transfer.wait_recv()

    def wait_send(transfers):
        for transfer in transfers:
            transfer.wait_send()

    def y_at(d):
        return lax.rem(y + d, 4)

    def x_at(d):
        return lax.rem(x + d, 4)

    def z_at(d):
        place = lax.rem(2 * r + zl + d, 4)
        return place // 2, lax.rem(place, 2)

    def along_x(d):
        return dev(r, y, zl, x_at(d), core)

    def along_y(d):
        return dev(r, y_at(d), zl, x, core)

    def along_z(d):
        rr, ll = z_at(d)
        return dev(rr, y, ll, x, core)

    def block_of(xx, kk):
        return xx * 2 + kk

    sib = dev(r, y, zl, x, 1 - core)
    diagonal = z == c
    plane = zl == core
    finals = []

    loads = []

    def load(index, src, dst):
        copy = pltpu.make_async_copy(src, dst, sends["load"].at[index])
        copy.start()
        loads.append(copy)

    for t in range(3):
        load(t, m_qkv.at[:, part(c + 8 * t, 128)], s.dk.at[128 * t : 128 * t + 128, :])
    for t in range(3, 7):
        load(t, m_in.at[:, part((2 * (t - 3) + core) * 4 + x, 128)], s.dk.at[128 * t : 128 * t + 128, :])
    for t in range(8):
        load(7 + t, m_out.at[part(x, 128), 128 * t : 128 * t + 128], s.dv.at[128 * t : 128 * t + 128, :])
        load(15 + t, m_dense.at[:, 128 * t : 128 * t + 128], s.dv.at[D + 128 * t : D + 128 * t + 128, :])

    barrier = pltpu.get_barrier_semaphore()
    peers = [along_x(1), along_x(2), along_x(3), sib]
    for dr in range(2):
        for dy in range(4):
            for dl in range(2):
                if dr or dy or dl:
                    peers.append(dev(lax.rem(r + dr, 2), y_at(dy), lax.rem(zl + dl, 2), x, core))
    for p in peers:
        pl.semaphore_signal(barrier, inc=1, device_id=p, device_id_type=MESH)

    own, inverse = unit_norm(tokens[...].astype(F32))
    s.n[rows(c), :] = own.astype(BF)
    first, second = lens[0, 0], lens[0, 1]
    second_start = (first + BLOCK - 1) // BLOCK * BLOCK

    def masked_cotangent():
        place = lax.broadcasted_iota(jnp.int32, (R, D), 0) + c * R
        valid = (place < first) | ((place >= second_start) & (place < second_start + second))
        return jnp.where(valid, cot[...].astype(F32), 0.0)

    s.back[rows(c), :] = masked_cotangent().astype(BF)
    s.small[pl.ds(z, 1)] = jnp.zeros((1, 16, 128), F32)
    s.small[pl.ds(z, 1), 0:13] = small_in[...].astype(BF).astype(F32)[None]
    for t in range(7):
        loads[t].wait()
        s.w1r[part(z, 128), 128 * t : 128 * t + 128] = s.dk[128 * t : 128 * t + 128, :].astype(BF)
    pl.semaphore_wait(barrier, len(peers))

    lb, rb, ob = block_of(x_at(3), core), block_of(x_at(1), core), block_of(x_at(2), core)

    def gather(name, buf):
        def half(b, h):
            return buf.at[pl.ds(pl.multiple_of(b * R + 128 * h, 128), 128), :]

        def whole(b):
            return buf.at[rows(b), :]

        def same(index, ref, target):
            return make(name, index, ref, ref, target)

        return [
            same(0, half(c, 0), along_x(1)),
            same(1, half(c, 1), along_x(3)),
            same(2, half(c, 1), along_x(1)),
            same(3, half(c, 0), along_x(3)),
            same(4, whole(c), sib),
            same(5, half(lb, 0), along_x(1)),
            same(6, half(rb, 1), along_x(3)),
            same(7, whole(lb), sib),
            same(8, whole(rb), sib),
            same(9, whole(ob), sib),
        ]

    def gather_forward(g, steps):
        for got, sent in steps:
            g[got].wait_recv()
            g[sent].start()

    to_chips, to_sibs = ((0, 5), (1, 6)), ((2, 7), (3, 8))

    def gather_across(g):
        g[5].wait_recv()
        g[6].wait_recv()
        g[9].start()

    def gather_done(g):
        wait_recv([g[4], g[7], g[8], g[9]])

    n_gather = gather("n", s.n)
    start(n_gather[:5])

    def spread(name, buf, row, same_send=None, same_recv=None, cross_send=None, cross_recv=None):
        out = []
        whole = buf.at[pl.ds(pl.multiple_of(row, 128), 128), :]
        for dy in (1, 3, 2):
            recv_if = same_recv(dy) if same_recv else None
            out.append(make(name, dy - 1, whole, whole, along_y(dy), same_send, recv_if))
        for dy in (0, 1, 3, 2):
            for h in range(2):
                ref = buf.at[pl.ds(pl.multiple_of(row + 64 * h, 64), 64), :]
                target = dev(r if h == 0 else 1 - r, y_at(dy), 1 - zl, x, core)
                recv_if = cross_recv(dy) if cross_recv else None
                out.append(make(name, 3 + 2 * dy + h, ref, ref, target, cross_send, recv_if))
        return out

    small_gather = []
    for dy in range(4):
        for dl in range(2):
            if dy or dl:
                target = dev(r, y_at(dy), lax.rem(zl + dl, 2), x, core)
                small_gather.append(make("small", 2 * dy + dl - 1, s.small.at[z], s.small.at[z], target))
    start(small_gather)
    w1_near, w1_far = [], []
    for dy in range(4):
        row = (y_at(4 - dy) * 2 + zl) * 128
        if dy:
            ref = s.w1r.at[part(z, 128), :]
            w1_near.append(make("w1", dy - 1, ref, ref, along_y(dy)))
        for h in range(2):
            ref = s.w1r.at[pl.ds(pl.multiple_of(row + 64 * h, 64), 64), :]
            target = dev(r if h == 0 else 1 - r, y, 1 - zl, x, core)
            w1_far.append(make("w1", 3 + 2 * dy + h, ref, ref, target))
    start([w1_near[0], w1_near[2], w1_near[1]])
    start(w1_far[0:2])

    lane_place = lax.broadcasted_iota(jnp.int32, (8, T), 1)
    in_first = lane_place < first
    in_second = (lane_place >= second_start) & (lane_place < second_start + second)
    s.low[...] = jnp.where(in_first, 0, jnp.where(in_second, second_start, lane_place))
    position = jnp.where(in_first, lane_place, jnp.where(in_second, lane_place - second_start, 0))
    entry = lax.broadcasted_iota(jnp.int32, (8, T), 0)
    frequency = jnp.zeros((8, T), F32)
    for t in range(8):
        frequency = jnp.where(entry == t, 10000.0 ** (-t / 8), frequency)
    turn = position.astype(F32) * frequency
    s.angle[0:8, :] = jnp.cos(turn)
    s.angle[8:16, :] = jnp.sin(turn)

    def tables(b):
        cs, sn = s.angle[0:8, rows(b)], s.angle[8:16, rows(b)]
        rest = jnp.zeros((32, R), F32)
        s.turn[rows(b), :] = jnp.concatenate([cs, cs, sn, sn, rest] * 2, axis=0).T

    each(tables)
    s.flatG[...] = jnp.zeros_like(s.flatG)
    s.smallG[...] = jnp.zeros_like(s.smallG)

    gather_forward(n_gather, to_chips)
    for dy in (1, 3, 2):
        w1_near[dy - 1].wait_recv()
        start(w1_far[2 * dy : 2 * dy + 2])
    gather_forward(n_gather, to_sibs)
    back_gather = gather("back", s.back)
    start(back_gather[:5])

    for t in range(7, 23):
        loads[t].wait()
    wo_row = 128 + y * 128
    wo_spread = spread("wo", s.w2, wo_row, plane, lambda dy: plane, plane, lambda dy: zl != core)

    def dense_from(dy):
        return lax.rem(y + 4 - dy, 4) == x

    wd_spread = spread(
        "wd", s.w2, 0, diagonal, lambda dy: dense_from(dy) & plane, diagonal, lambda dy: dense_from(dy) & (zl != core))

    @pl.when(plane)
    def _():
        for t in range(8):
            cols = slice(128 * t, 128 * t + 128)
            s.w2[pl.ds(pl.multiple_of(wo_row, 128), 128), cols] = s.dv[128 * t : 128 * t + 128, :].astype(BF)

    @pl.when(diagonal)
    def _():
        for t in range(8):
            s.w2[0:128, 128 * t : 128 * t + 128] = s.dv[D + 128 * t : D + 128 * t + 128, :].astype(BF)

    s.dk[...] = jnp.zeros_like(s.dk)
    s.dv[...] = jnp.zeros_like(s.dv)
    s.dqT[...] = jnp.zeros_like(s.dqT)
    start(wd_spread)
    start(wo_spread)

    wait_recv(small_gather)
    for t in range(8):
        s.flat[13 * t : 13 * t + 13, :] = s.small[t, 0:13, :]
    s.cols[...] = s.flat[0:32, :].T
    wait_recv(w1_far)

    def line(at):
        return jnp.concatenate([s.flat[at + t : at + t + 1, :] for t in range(8)], axis=1)

    shifts = jnp.concatenate([line(8), line(24), jnp.zeros((6, D), F32)], axis=0).astype(BF)
    turned = nn(shifts, s.w1r[...])
    for t in range(3):
        cols = slice(128 * t, 128 * t + 128)
        s.bias[0:1, cols] = turned[0:1, cols] + s.flat[pl.ds(32 + 8 * t + c, 1), :]
    for t in range(4):
        cols = slice(QKV + 128 * t, QKV + 128 * t + 128)
        s.bias[0:1, cols] = turned[1:2, cols] + s.flat[pl.ds(72 + (2 * t + core) * 4 + x, 1), :]
    for t in range(8):
        sl = slice(128 * t, 128 * t + 128)
        s.w1[sl, :QKV] = (s.w1r[sl, :QKV].astype(F32) * s.cols[:, t : t + 1]).astype(BF)
        s.w1[sl, QKV:] = (s.w1r[sl, QKV:].astype(F32) * s.cols[:, 16 + t : 17 + t]).astype(BF)

    wait_recv(n_gather[4:5])

    def project_turn(t):
        p, q = t // 2, lax.rem(t, 2)

        @pl.when(t == 4)
        def _():
            gather_across(n_gather)
            wait_recv(n_gather[7:9])

        @pl.when(t == 6)
        def _():
            wait_recv(n_gather[9:])

        middle = lax.rem((p + 1) // 2, 2)
        dx = middle * (3 - 2 * q) + (1 - middle) * 2 * (p // 3)
        dk = middle * (p - 1) + (1 - middle) * q
        project(block_of(x_at(dx), lax.rem(core + dk, 2)), s)

    each(project_turn)
    gather_forward(back_gather, to_chips)

    class Owner:
        def __init__(self, buf, kind):
            self.buf, self.kind = buf, kind
            self.sib_slots, self.near_slots = getattr(s, "sib" + kind), getattr(s, "near" + kind)

        def to_sibling(self, xx):
            return make("sib" + self.kind, xx, self.buf.at[rows(block_of(xx, 1 - core)), :], self.sib_slots.at[xx], sib)

        def near(self, xx, d):
            return make(
                "near" + self.kind, d - 1, self.buf.at[rows(block_of(xx, core)), :], self.near_slots.at[d - 1],
                dev(r, y, zl, xx, core))

        def add(self, xx):
            self.to_sibling(xx).wait_recv()
            here = rows(block_of(xx, core))
            mine = self.buf[here, :].astype(F32) + self.sib_slots[pl.ds(xx, 1)][0].astype(F32)
            self.buf[here, :] = mine.astype(BF)
            pl.when(xx != x)(lambda: self.near(xx, lax.rem(x + 4 - xx, 4)).start())

        def total(self):
            total = self.buf[rows(c), :].astype(F32)
            for d in (1, 3, 2):
                self.near(x_at(4 - d), d).wait_recv()
                total = total + self.near_slots[d - 1].astype(F32)
            return total

        def drain(self):
            for xx in range(4):
                self.to_sibling(xx).wait_send()
            for d in (1, 2, 3):
                self.near(x_at(4 - d), d).wait_send()

    out_owner = Owner(s.n, "O")
    e_owner = Owner(s.back, "E")

    def down(i):
        s.n[rows(i), :] = nn(s.A[rows(i), :], s.w2[...]).astype(BF)

    def attend_turn(i):
        pl.when(i == 2)(lambda: gather_forward(back_gather, to_sibs))
        attend(i, s)

    def down_first(xx):
        down(block_of(xx, 1 - core))
        out_owner.to_sibling(xx).start()

    each(attend_turn, 0, 4)
    gather_across(back_gather)
    wait_send(n_gather)
    wait_recv(wd_spread)
    wait_recv(wo_spread)
    each(down_first, 0, 4)
    each(lambda xx: down(block_of(xx, core)), 0, 4)
    gather_done(back_gather)
    each(lambda b: pull_down(b, s), 0, 4)
    each(out_owner.add, 0, 4)
    each(lambda b: pull_down(b, s), 4, 8)

    def grad_down(t):
        cols = part(t, 256)
        g = nn(s.AT[...], s.back[:, cols]).astype(BF)
        for h in range(2):
            s.gd[h, :, cols] = g[64 * h : 64 * h + 64]
            for yy in range(4):
                s.go[yy, h, :, cols] = g[128 + 128 * yy + 64 * h : 192 + 128 * yy + 64 * h]

    each(grad_down, 0, 4)

    def down_grads_out():
        out = [make("yo", d - 1, s.go.at[y_at(d)], s.yo.at[d - 1], along_y(d)) for d in (1, 3, 2)]
        for d in (1, 3, 2):
            rr, ll = z_at(d)
            out.append(make("zd", d - 1, s.gd.at[rr], s.zd.at[d - 1], along_z(d), ll == core, plane))
        return out

    down_sends = start(down_grads_out())

    def z_sends(name, src, slots):
        return [make(name, d - 1, src.at[2 * z_at(d)[0] + z_at(d)[1]], slots.at[d - 1], along_z(d)) for d in (1, 3, 2)]

    def y_sends(name, src, slots):
        return [make(name, d - 1, src.at[y_at(d)], slots.at[d - 1], along_y(d)) for d in (1, 3, 2)]

    def z_sum(transfers, src, slots, out):
        wait_recv(transfers)
        mine = src[pl.ds(2 * r + zl, 1)][0].astype(F32)
        for d in range(3):
            mine = mine + slots[d].astype(F32)
        out[...] = mine.astype(out.dtype)

    def y_sum(transfers, src, slots):
        wait_recv(transfers)
        mine = src[pl.ds(y, 1)][0].astype(F32)
        for d in range(3):
            mine = mine + slots[d].astype(F32)
        return mine

    def grad_up(lo, hi, place, gain_at, shift_at):
        g = nn(s.nT[...], s.dP[:, lo:hi])
        total = jnp.sum(s.dP[:, lo:hi].astype(F32), axis=0, keepdims=True)
        for t in range(8):
            sl = slice(128 * t, 128 * t + 128)
            full = g[sl] * s.cols[:, gain_at + t : gain_at + t + 1] + s.cols[:, shift_at + t : shift_at + t + 1] * total
            for h in range(2):
                place(2 * h + t % 2, t // 2, full[64 * h : 64 * h + 64].astype(BF))
        return g, total

    def norm_sums(lo, hi, g, total):
        gains, moves = [], []
        for t in range(8):
            sl = slice(128 * t, 128 * t + 128)
            w = s.w1r[sl, lo:hi].astype(F32)
            gains.append(jnp.sum(w * g[sl], axis=1, keepdims=True))
            moves.append(jnp.sum(w * total, axis=1, keepdims=True))
        return jnp.concatenate(gains, axis=1), jnp.concatenate(moves, axis=1)

    def place_in(at):
        def place(p4, yy, value):
            s.gi[p4, yy, :, at : at + 256] = value

        return place

    def place_q(p4, yy, value):
        s.gq[p4, yy] = value

    def place_v(p4, yy, value):
        s.gv[yy, p4] = value

    g_a, total_a = grad_up(QKV, QKV + 256, place_in(0), 16, 24)
    g_b, total_b = grad_up(QKV + 256, WIDE, place_in(256), 16, 24)
    zi_sends = start(z_sends("zi", s.gi, s.zi))
    gain_a, move_a = norm_sums(QKV, QKV + 256, g_a, total_a)
    gain_b, move_b = norm_sums(QKV + 256, WIDE, g_b, total_b)
    s.flatG[16:32, :] = jnp.concatenate([gain_a + gain_b, move_a + move_b], axis=1).T
    for t in range(4):
        total = total_a if t < 2 else total_b
        at = 128 * (t % 2)
        s.flatG[pl.ds(72 + (2 * t + core) * 4 + x, 1), :] = total[:, at : at + 128]
    back_sum = jnp.sum(s.back[rows(c), :].astype(F32), axis=0, keepdims=True)
    for t in range(8):
        s.flatG[56 + t : 57 + t, :] = back_sum[:, 128 * t : 128 * t + 128]
        s.flatG[64 + t : 65 + t, :] = back_sum[:, 128 * t : 128 * t + 128]

    wait_send(back_gather)

    def turn_x(t):
        return 3 - lax.rem(t, 4)

    def turn_core(t):
        return lax.rem(turn_x(t) + t // 4, 2)

    def back_sum(t):
        @pl.when(turn_core(t) == core)
        def _():
            e_owner.add(turn_x(t))

    def back_step(t):
        b = block_of(turn_x(t), turn_core(t))
        late = t // 4
        row_pairs = (4 - t) * (1 - late) + (4 - t // 2) * late
        column_pairs = ((t + 1) // 2) * (1 - late)
        each(lambda l: tile_back(b, R, late + (2 + 2 * late) * l, PAIR, s), 0, row_pairs)
        each(lambda l: tile_back(5 - 4 * (column_pairs - 1) + 4 * l, PAIR, b, R, s), 0, column_pairs)
        finish_back(b, s)

        @pl.when(turn_core(t) != core)
        def _():
            e_owner.to_sibling(turn_x(t)).start()

        pl.when(t > 0)(lambda: back_sum(t - 1))

    def final_gather(name, buf, out, slot, source=None):
        def has(xx, kk):
            return source(xx, kk) if source else None

        def at(xx, kk, *h):
            return slot(out, xx, kk, *h)

        local = pltpu.make_async_copy(buf, at(x, core), sends[name].at[8])
        first_hop = [
            make(name, n, buf, at(x, core), along_x(d), has(x, core), has(x_at(4 - d), core)) for n, d in ((0, 1), (1, 3))]
        first_hop.append(make(name, 2, buf, at(x, core), sib, has(x, core), has(x, 1 - core)))
        onward, second_hop = [], []
        for n, d in ((0, 1), (1, 3)):
            xx = x_at(4 - d)
            ref = at(xx, core, n)
            onward.append(make(name, 3 + n, ref, ref, along_x(d), has(xx, core), has(x_at(2), core)))
        for n, d in ((5, 3), (6, 1), (7, 2)):
            ref = at(x_at(d), core)
            second_hop.append(make(name, n, ref, ref, sib, has(x_at(d), core), has(x_at(d), 1 - core)))
        return Transfer(local, has(x, core)), first_hop, second_hop, onward

    def final_start(g):
        g[0].start()
        start(g[1])

    def final_forward(g):
        for n in range(2):
            g[1][n].wait_recv()
            g[3][n].start()
            g[2][n].start()

    def final_across(g):
        wait_recv(g[3])
        g[2][2].start()

    def final_finish(g):
        g[0].only(g[0].send_if, g[0].copy.wait)
        g[1][2].wait_recv()
        wait_recv(g[2])
        finals.extend(g[1] + g[2] + g[3])

    yi_sends = y_sends("yi", s.ti, s.yi)
    second_sends = []
    for d in (1, 3, 2):
        rr, ll = z_at(d)
        second_sends.append(make("zo", d - 1, s.to.at[rr], s.zo.at[d - 1], along_z(d), ll == core, plane))

    def to_diagonal(d):
        return make("yd", d - 1, s.td, s.yd.at[d - 1], along_y(d), plane & (y_at(d) == x), diagonal)

    second_dense = [to_diagonal(d) for d in (1, 3, 2)]

    def early_second():
        z_sum(zi_sends, s.gi, s.zi, s.ti)
        start(yi_sends)
        wait_recv(down_sends)
        total = s.go[pl.ds(y, 1)][0].astype(F32) + s.yo[0].astype(F32) + s.yo[1].astype(F32) + s.yo[2].astype(F32)
        s.to[...] = total.astype(BF)

        @pl.when(plane)
        def _():
            mine = s.gd[pl.ds(r, 1)][0].astype(F32)
            for d in range(3):
                mine = mine + s.zd[d].astype(F32)
            s.td[...] = mine.astype(BF)

        start(second_sends)
        start(second_dense)

    other = dev(1 - r, y, zl, x, core)

    def halves(name, buf, condition=None):
        ref = buf.at[r] if len(buf.shape) == 3 else buf.at[:, r]
        return make(name, 0, ref, ref, other, condition, condition)

    def in_blocks(value, buf):
        for t in range(buf.shape[0]):
            buf[t, pl.ds(r, 1)] = value[:, 128 * t : 128 * t + 128].astype(BF)[None]

    early = [halves("ri", s.fi), halves("ro", s.fo, plane), halves("rd", s.fd, diagonal)]

    def early_whole():
        in_blocks(y_sum(yi_sends, s.ti, s.yi), s.fi)
        wait_recv(second_sends)
        wait_recv(second_dense)

        @pl.when(plane)
        def _():
            mine = s.to[pl.ds(r, 1)][0].astype(F32)
            for d in range(3):
                mine = mine + s.zo[d].astype(F32)
            s.fo[pl.ds(r, 1)] = mine.astype(BF)[None]

        @pl.when(diagonal)
        def _():
            mine = s.td[...].astype(F32)
            for d in range(3):
                mine = mine + s.yd[d].astype(F32)
            s.fd[pl.ds(r, 1)] = mine.astype(BF)[None]
        start(early)

    g_in = final_gather("ai", s.fi, o_in, lambda out, xx, kk, *h: out.at[(slice(None), kk, xx, *h)])
    g_out = final_gather("ao", s.fo, o_out, lambda out, xx, kk, *h: out.at[(xx, *h)], lambda xx, kk: zl == kk)
    g_dense = final_gather("ad", s.fd, o_dense, lambda out, xx, kk, *h: out.at[h] if h else out, lambda xx, kk: (zl == kk) & (y == xx))

    def early_gather():
        wait_recv(early)
        for g in (g_in, g_out, g_dense):
            final_start(g)

    def back_turn(t):
        back_step(t)
        pl.when(t == EARLY_SECOND)(early_second)
        pl.when(t == EARLY_WHOLE)(early_whole)
        pl.when(t == EARLY_GATHER)(early_gather)

    each(back_turn)
    back_sum(7)
    g_q, total_q = grad_up(0, 256, place_q, 0, 8)
    zq_sends = start(z_sends("zq", s.gq, s.zq))
    g_v, total_v = grad_up(256, QKV, place_v, 0, 8)
    yv_sends = start(y_sends("yv", s.gv, s.yv))
    gain_q, move_q = norm_sums(0, 256, g_q, total_q)
    gain_v, move_v = norm_sums(256, QKV, g_v, total_v)
    s.flatG[0:16, :] = jnp.concatenate([gain_q + gain_v, move_q + move_v], axis=1).T
    s.flatG[pl.ds(32 + c, 1), :] = total_q[:, 0:128]
    s.flatG[pl.ds(40 + c, 1), :] = total_q[:, 128:256]
    s.flatG[pl.ds(48 + c, 1), :] = total_v
    for t in range(8):
        s.smallG[t % 2, t // 2, 0:13, :] = s.flatG[13 * t : 13 * t + 13, :]
    small_z = start([make("smallZ", d - 1, s.smallG.at[z_at(d)[1]], s.smallZ.at[d - 1], along_z(d)) for d in (1, 3, 2)])

    total = out_owner.total()
    bias = jnp.concatenate([s.flat[56 + t : 57 + t, :] + s.flat[64 + t : 65 + t, :] for t in range(8)], axis=1)
    block_out[...] = (tokens[...].astype(F32) + bias + total).astype(BF)

    s.tv[...] = y_sum(yv_sends, s.gv, s.yv).astype(BF)
    zv_sends = start(z_sends("zv", s.tv, s.zv))
    z_sum(zq_sends, s.gq, s.zq, s.tq)
    yq_sends = start(y_sends("yq", s.tq, s.yq))
    wait_recv(small_z)
    s.smallT[...] = s.smallG[pl.ds(zl, 1)][0] + s.smallZ[0] + s.smallZ[1] + s.smallZ[2]
    small_y = start(y_sends("smallY", s.smallT, s.smallY))
    wait_recv(zv_sends)
    mine = s.tv[pl.ds(2 * r + zl, 1)][0].astype(F32)
    for d in range(3):
        mine = mine + s.zv[d].astype(F32)
    in_blocks(jnp.concatenate([y_sum(yq_sends, s.tq, s.yq), mine], axis=1), s.fq)
    late = start([halves("rq", s.fq)])
    s.smallU[...] = y_sum(small_y, s.smallT, s.smallY)
    small_x = start([make("smallX", d - 1, s.smallU, s.smallX.at[d - 1], along_x(d)) for d in (1, 3, 2)])

    wait_recv(late)
    g_qkv = final_gather("aq", s.fq, o_qkv, lambda out, xx, kk, *h: out.at[(slice(None), block_of(xx, kk), *h)])
    final_start(g_qkv)
    final_forward(g_in)
    final_forward(g_out)
    final_forward(g_dense)

    e = e_owner.total()
    own, inverse = unit_norm(tokens[...].astype(F32))
    mean_e = jnp.mean(e, axis=-1, keepdims=True)
    mean_en = jnp.mean(e * own, axis=-1, keepdims=True)
    tokens_grad[...] = masked_cotangent() + inverse * (e - mean_e - own * mean_en)

    wait_recv(small_x)
    s.smallV[...] = s.smallU[...] + s.smallX[0] + s.smallX[1] + s.smallX[2]
    small_s = start([make("smallS", 0, s.smallV, s.smallS, sib)])
    final_forward(g_qkv)
    for g in (g_in, g_out, g_dense, g_qkv):
        final_across(g)
    wait_recv(small_s)
    o_small[...] = s.smallV[...] + s.smallS[...]

    for g in (g_in, g_out, g_dense, g_qkv):
        final_finish(g)
    out_owner.drain()
    e_owner.drain()
    for group in (
        finals, small_gather, w1_near, w1_far, wo_spread, wd_spread, down_sends, zi_sends, yi_sends, second_sends, second_dense,
        early, zq_sends, yq_sends, yv_sends, zv_sends, late, small_z, small_y, small_x, small_s,
    ):
        wait_send(group)


def block_step(tokens, cot, lens, small_in, m_qkv, m_dense, m_in, m_out):
    vmem = pl.BlockSpec(memory_space=pltpu.VMEM)
    hbm = pl.BlockSpec(memory_space=pl.ANY)
    shapes = [
        jax.ShapeDtypeStruct((R, D), BF), jax.ShapeDtypeStruct((R, D), F32),
        jax.ShapeDtypeStruct((3, 8, 2, 64, 128), BF), jax.ShapeDtypeStruct((4, 2, 4, 2, 64, 128), BF),
        jax.ShapeDtypeStruct((4, 2, 64, D), BF), jax.ShapeDtypeStruct((2, 64, D), BF),
        jax.ShapeDtypeStruct((16, 128), F32),
    ]
    scratch = [pltpu.VMEM(shape, kind) for shape, kind in VMEM_SHAPES.values()]
    scratch += [pltpu.SemaphoreType.DMA((count,)) for count in SEMS.values()] * 2
    return pl.pallas_call(
        kernel,
        out_shape=shapes,
        in_specs=[vmem, vmem, pl.BlockSpec(memory_space=pltpu.SMEM), vmem, hbm, hbm, hbm, hbm],
        out_specs=[vmem, vmem, hbm, hbm, hbm, hbm, vmem],
        scratch_shapes=scratch,
        compiler_params=pltpu.CompilerParams(
            collective_id=0, has_side_effects=True, vmem_limit_bytes=VMEM_LIMIT),
        name="block_step",
    )(tokens, cot, lens, small_in, m_qkv, m_dense, m_in, m_out)


VMEM_LIMIT = 60 * 2**20


def adam_update(master, first_old, second_old, gradient, rate):
    first_new = BETA_ONE * first_old + (1.0 - BETA_ONE) * gradient
    second_new = BETA_TWO * second_old + (1.0 - BETA_TWO) * gradient * gradient
    first_hat = first_new / (1.0 - BETA_ONE**STEP)
    second_hat = second_new / (1.0 - BETA_TWO**STEP)
    updated = master - rate * (first_hat / (jnp.sqrt(second_hat) + ADAM_EPS) + DECAY * master)
    return gradient, second_new, updated


def adam_chunks():
    cols = [(0, b, 6) for b in range(0, 24, 6)] + [(2, b, 8) for b in range(0, 32, 8)]
    out = [(t, (slice(None), slice(128 * b, 128 * (b + n))), slice(b, b + n)) for t, b, n in cols]
    out += [(3, slice(128 * b, 128 * b + 128), slice(128 * b, 128 * b + 128)) for b in range(4)]
    return out + [(1, slice(None), slice(None)), (4, slice(None), slice(0, 13))]


def adam_kernel(*refs):
    grads, state, given, outs, passed = refs[:5], refs[5:20], refs[20:22], refs[22:37], refs[37:39]
    grad_vmem, state_vmem, given_vmem = refs[39:44], refs[44:59], refs[59:61]
    in_sem, out_sem, given_sem, passed_sem = refs[61:65]
    chunks = adam_chunks()
    loads, stores = [], []
    for n, (t, at, grad_at) in enumerate(chunks):
        group = [pltpu.make_async_copy(grads[t].at[grad_at], grad_vmem[t].at[grad_at], in_sem.at[n, 3])]
        for o in range(3):
            k = 5 * o + t
            group.append(pltpu.make_async_copy(state[k].at[at], state_vmem[k].at[at], in_sem.at[n, o]))
        for copy in group:
            copy.start()
        loads.append(group)
    givens = [pltpu.make_async_copy(given[n], given_vmem[n], given_sem.at[n]) for n in range(2)]
    for copy in givens:
        copy.start()
    for n, (t, at, grad_at) in enumerate(chunks):
        for copy in loads[n]:
            copy.wait()
        bufs = [state_vmem[5 * o + t] for o in range(3)]

        def step(where, gradient, t=t, bufs=bufs):
            master, first, second = (buf[where] for buf in bufs)
            _, renewed, updated = adam_update(master, first, second, gradient, RATES[t])
            bufs[0][where], bufs[1][where], bufs[2][where] = updated, gradient, renewed

        if t in (0, 2):
            for b in range(grad_at.start, grad_at.stop):
                step((slice(None), slice(128 * b, 128 * b + 128)), grad_vmem[t][b].astype(F32))
        else:
            step((at, slice(None)), grad_vmem[t][grad_at, :].astype(F32))
        for o, buf in ((0, bufs[1]), (1, bufs[2]), (2, bufs[0])):
            copy = pltpu.make_async_copy(buf.at[at], outs[5 * o + t].at[at], out_sem.at[n, o])
            copy.start()
            stores.append(copy)
    for n in range(2):
        givens[n].wait()
        copy = pltpu.make_async_copy(given_vmem[n], passed[n], passed_sem.at[n])
        copy.start()
        stores.append(copy)
    for copy in stores:
        copy.wait()


def adam_step(grads, state, given):
    hbm = pl.BlockSpec(memory_space=pl.ANY)
    count = len(adam_chunks())
    return pl.pallas_call(
        adam_kernel,
        out_shape=[jax.ShapeDtypeStruct(a.shape, a.dtype) for a in (*state, *given)],
        in_specs=[hbm] * 22,
        out_specs=[hbm] * 17,
        scratch_shapes=[pltpu.VMEM(a.shape, a.dtype) for a in (*grads, *state, *given)]
        + [pltpu.SemaphoreType.DMA(shape) for shape in ((count, 4), (count, 3), (2,), (2,))],
        compiler_params=pltpu.CompilerParams(vmem_limit_bytes=VMEM_LIMIT),
        name="adam_step",
    )(*grads, *state, *given)


def per_device(tokens, cotangent, seq_lengths, *state):
    state = [a.reshape(13, 128) if a.ndim == 1 else a for a in state]
    block_out, tokens_grad, g_qkv, g_in, g_out, g_dense, g_small = block_step(
        tokens, cotangent, seq_lengths, state[4], *state[:4])
    grads = [
        g_qkv.reshape(24, 128, 128), g_dense.reshape(128, D), g_in.reshape(32, 128, 128), g_out.reshape(512, D), g_small]
    *results, block_out, tokens_grad = adam_step(grads, state, [block_out, tokens_grad])
    return (block_out, tokens_grad, *(a.reshape(-1) if a.shape[0] == 13 else a for a in results))


def solution(mesh):
    seq = P(("rep", "zero", "ctx"), None)
    state = (P("zero", None),) * 4 + (P("zero"),)
    return jax.shard_map(
        per_device,
        mesh=mesh,
        in_specs=(seq, seq, P(("rep", "zero"), None)) + state * 3,
        out_specs=(seq, seq) + state * 3,
        check_vma=False,
    )
```
